128 devices in a mesh: stn: 8 (over x_lo, y), src: 16 (over z, x_hi, core).
Axes of the slice: x: 4 (x_hi: 2, x_lo: 2; x = x_hi * 2 + x_lo), y: 4, z: 4, core: 2. Of those that a mesh axis runs over, the one named last changes fastest.
Arguments:
- beam_jones: bfloat16 [8, 512, 16384], P(None, 'stn', 'src'), may hold values from -3 to 3
- source_lm: float32 [2, 16384], P(None, 'src'), may hold values from -0.3 to 0.3
- source_flux: float32 [16384], P('src'), may hold values from 0.3 to 3
- live_counts: int32 [16], P('src'), may hold values from 1 to 1024, 9216 in all
- station_uvw: float32 [3, 512], replicated, may hold values from -400 to 400
- chan_scale: float32 [4], replicated, may hold values from 0.9 to 1.1
- block_pairs: int32 [136, 2], P('stn'), may hold values from 0 to 15, as said below
Outputs:
- visibility: float32 [136, 32768], P('stn', 'src')
The draws below stay inside these ranges and needn't reach their ends.
Inputs may be any that keep to these rules, and one draw needn't show every extreme that they name: `block_pairs`: each row holds two station blocks i <= j; every such pair of the 16 blocks appears exactly once. `live_counts`: some shard is full (1024 live); the counts sum to 9216.
All inputs are finite; a program needn't handle non-finite values.
Results may differ from the reference program's by a relative error of at most 0.00081.
Values may be sent and summed in bfloat16 or wider, within the bound.
No kernel may reach another device: no remote copies, remote signals or barrier semaphores. Data moves between devices by JAX's collectives and lax.ppermute only.
A program may use at most 128 MiB of HBM per device.

```python
import math
import jax
import jax.numpy as jnp
import numpy as np
from jax import lax

STATIONS = 512
CHANNELS = 4
NBLK = 16
SRC_DEV = 1024
SHARDS = 16
SOURCES = 16384
NPAIR = 136
N_SRC = 16


def draw_block_pairs(key, part):
    key = jax.random.fold_in(key, 7)
    upper_rows, upper_cols = np.triu_indices(NBLK)
    table = jnp.stack([jnp.asarray(upper_rows), jnp.asarray(upper_cols)], axis=1).astype(jnp.int32)
    shuffle = jax.random.permutation(key, NPAIR)
    return table[shuffle]


def block_scale(own_key, extent, cuts, low, largest):
    def one(dim, blocks):
        draws = jax.random.uniform(jax.random.fold_in(jax.random.fold_in(own_key, 6), dim), (blocks,), jnp.float32, low / len(cuts), largest / len(cuts))
        return jnp.repeat(jnp.exp(draws), extent[dim] // blocks).reshape((-1,) + (1,) * (len(extent) - dim - 1))

    level = one(*cuts[0])
    for cut in cuts[1:]:
        level = level * one(*cut)
    return level


def split_up(count, total, most, slope):
    loads = [(1 << 20) // math.isqrt(grade ** slope) + 1 for grade in range(2, count + 1)]
    surplus, counts = total - most - (count - 1), [1] * (count - 1)
    while surplus > 0:
        free = [i for i in range(count - 1) if counts[i] < most]
        whole, remaining = sum([loads[i] for i in free]), surplus
        for i in free:
            more = min(most - counts[i], max(1, remaining * loads[i] // whole), surplus)
            counts[i] = counts[i] + more
            surplus = surplus - more
    return np.array([most] + counts)


def uneven_parts(own_key, number_of, total, limit, lean):
    if number_of == 2:
        one = jax.random.randint(own_key, (), max(1, total - limit), min(limit, total - 1) + 1)
        return jnp.stack([one, total - one])
    tallies = jnp.asarray(split_up(number_of, total, limit, lean), jnp.int32)
    couples = (number_of - 1) // 2
    donor, taker = tallies[1:1 + 2 * couples:2], tallies[2:2 + 2 * couples:2]
    margin = jnp.minimum(donor - 1, limit - taker)
    shifted = jax.random.randint(jax.random.fold_in(own_key, 1), (couples,), 0, 1 << 20) % (margin + 1)
    tallies = tallies.at[1:1 + 2 * couples:2].set(donor - shifted).at[2:2 + 2 * couples:2].set(taker + shifted)
    return tallies[jax.random.permutation(jax.random.fold_in(own_key, 2), number_of)]


def gaussian(own_key, shape, spread, limit, pieces=(), kind=jnp.bfloat16):
    drawn = jax.random.normal(own_key, shape, jnp.float32) * spread
    if len(pieces) > 0:
        drawn = block_scale(own_key, shape, pieces, -0.22, 0.18) * drawn
    return jnp.clip(drawn, min=-limit, max=limit).astype(kind)


def setup_inputs(seed: int = 0) -> dict:
    key_of = jax.random.split(jax.random.key(seed), 8)
    beam_jones = gaussian(key_of[0], (8, STATIONS, SOURCES), 0.5, 3.0, ((1, 8), (2, 16)))
    source_lm = jnp.clip(jax.random.uniform(key_of[1], (2, SOURCES), jnp.float32, -0.3, 0.3) * block_scale(key_of[1], (2, SOURCES), ((1, 16),), -0.4, 0.0), -0.3, 0.3)
    source_flux = jnp.clip(jnp.exp(math.log(3.0) - 2.3025851 * jax.random.uniform(key_of[2], (SOURCES,), jnp.float32) ** block_scale(key_of[2], (SOURCES,), ((0, 16),), -0.2, 0.2)), 0.3, 3.0)
    live_counts = uneven_parts(key_of[3], SHARDS, SRC_DEV * SHARDS * 9 // 16, SRC_DEV, 2).astype(jnp.int32)
    station_uvw = gaussian(key_of[4], (3, STATIONS), 100.0, 400.0, (), jnp.float32)
    chan_scale = jnp.clip(jax.random.uniform(key_of[5], (CHANNELS,), jnp.float32, 0.9, 1.1), 0.9, 1.1)
    block_pairs = draw_block_pairs(jax.random.fold_in(key_of[7], 71), 0)
    return {"beam_jones": beam_jones, "source_lm": source_lm, "source_flux": source_flux, "live_counts": live_counts, "station_uvw": station_uvw, "chan_scale": chan_scale, "block_pairs": block_pairs}


def beam_field(jones_slab, sky_lm, weights, station_uvw, chan_scale):
    dir_l = sky_lm[0]
    dir_m = sky_lm[1]
    w_depth = jnp.sqrt(1.0 - dir_l * dir_l - dir_m * dir_m) - 1.0
    geometry = station_uvw[0][:, None] * dir_l[None, :] + station_uvw[1][:, None] * dir_m[None, :] + station_uvw[2][:, None] * w_depth[None, :]
    phases = 2.0 * math.pi * chan_scale[:, None, None] * geometry[None]
    cosine = jnp.cos(phases)[:, :, None, None, :]
    sine_part = jnp.sin(phases)[:, :, None, None, :]
    components = jones_slab.astype(jnp.float32).reshape(2, 2, 2, jones_slab.shape[1], jones_slab.shape[2])
    real_jones = jnp.transpose(components[0], (2, 0, 1, 3))[None]
    imag_jones = jnp.transpose(components[1], (2, 0, 1, 3))[None]
    amplitude = jnp.sqrt(weights)
    field_re = (real_jones * cosine + imag_jones * sine_part) * amplitude
    field_im = (imag_jones * cosine - real_jones * sine_part) * amplitude
    out_shape = (chan_scale.shape[0], 2 * jones_slab.shape[1], 2 * jones_slab.shape[2])
    return (field_re.reshape(out_shape).astype(jnp.bfloat16), field_im.reshape(out_shape).astype(jnp.bfloat16))

def reference(beam_jones, source_lm, source_flux, live_counts, station_uvw, chan_scale, block_pairs):
    slot_index = jnp.arange(SOURCES, dtype=jnp.int32)
    live_mask = slot_index % SRC_DEV < live_counts[slot_index // SRC_DEV]
    weights = source_flux * live_mask.astype(jnp.float32) / math.sqrt(SOURCES)
    channels = chan_scale.shape[0]

    def gram(left, right):
        return jnp.einsum('cxk,cyk->cxy', left, right, precision=lax.Precision.HIGHEST)

    def accumulate(running, shard_index):
        start_at = (shard_index * SRC_DEV).astype(jnp.int32)
        slab = lax.dynamic_slice_in_dim(beam_jones, start_at, SRC_DEV, 2)
        sky_part = lax.dynamic_slice_in_dim(source_lm, start_at, SRC_DEV, 1)
        share = lax.dynamic_slice_in_dim(weights, start_at, SRC_DEV, 0)
        field_re, field_im = beam_field(slab, sky_part, share, station_uvw, chan_scale)
        field_re = field_re.astype(jnp.float32)
        field_im = field_im.astype(jnp.float32)
        real_sum = running[0] + (gram(field_re, field_re) + gram(field_im, field_im))
        imag_sum = running[1] + (gram(field_im, field_re) - gram(field_re, field_im))
        return ((real_sum, imag_sum), None)
    start_zero = jnp.zeros((channels, 2 * STATIONS, 2 * STATIONS), jnp.float32)
    totals, unused = lax.scan(accumulate, (start_zero, start_zero), jnp.arange(N_SRC, dtype=jnp.int32))
    block_rows = 2 * STATIONS // NBLK
    real_blocks = totals[0].reshape(channels, NBLK, block_rows, NBLK, block_rows)
    imag_blocks = totals[1].reshape(channels, NBLK, block_rows, NBLK, block_rows)
    left_block = block_pairs[:, 0]
    right_block = block_pairs[:, 1]
    real_pick = real_blocks[:, left_block, :, right_block, :]
    imag_pick = imag_blocks[:, left_block, :, right_block, :]
    return jnp.stack([real_pick, imag_pick], axis=2).reshape(NPAIR, -1)
```

```python
import functools
import math

import jax
import jax.numpy as jnp
import numpy as np
from jax import lax
from jax.experimental import pallas as pl
from jax.experimental.pallas import tpu as pltpu
from jax.sharding import PartitionSpec as P

NBLK = 16
STN = 8
PAIRS_DEV = 17
LANES = 128
JROWS = 512
EXTRA = 16
ROWS = JROWS + EXTRA
KCOL = 1024
SEND_SCALE = 1.0

TWO_PI_HI = 6.28125
TWO_PI_LO = 2.0 * math.pi - 6.28125
def _fit(fun, power, terms):
    x = np.cos(np.pi * (np.arange(4000) + 0.5) / 4000) * (math.pi * 1.001)
    cols = np.stack([x ** (2 * n + power) for n in range(terms)], 1)
    scale = np.abs(cols).max(0)
    sol, *_ = np.linalg.lstsq(cols / scale, fun(x), rcond=None)
    return [float(v) for v in sol / scale]


SIN_TERMS = _fit(np.sin, 1, 7)
COS_TERMS = _fit(np.cos, 0, 8)


def horner(square, terms):
    total = jnp.full_like(square, terms[-1])
    for term in terms[-2::-1]:
        total = total * square + term
    return total


def three(rows, at):
    return (rows[at : at + 1] + rows[at + 1 : at + 2]) + rows[at + 2 : at + 3]


def field_slab(pieces, uvw_ref, scale, kappa, g_ref, l_ref):
    for h, parts in enumerate(pieces):
        info = parts[0][0][0, JROWS:ROWS, :].astype(jnp.float32)
        dir_l, dir_m, depth, amp = (three(info, 3 * n) for n in range(4))
        for ref, first in parts:
            count = ref.shape[0]

            def step(at, carry, ref=ref, first=first):
                blk = 2 * first + at
                row = pl.multiple_of(32 * (at % 2), 32)
                here = pl.ds(pl.multiple_of(32 * blk, 32), 32)
                geometry = (
                    uvw_ref[0, here, :] * dir_l + uvw_ref[1, here, :] * dir_m
                ) + uvw_ref[2, here, :] * depth
                phase = scale * geometry
                turns = jnp.round(phase * (0.5 / math.pi))
                angle = (phase - turns * TWO_PI_HI) - turns * TWO_PI_LO
                square = angle * angle
                sine = horner(square, SIN_TERMS) * (angle * amp)
                cosine = horner(square, COS_TERMS) * amp
                for a in range(2):
                    g_rows = pl.ds(pl.multiple_of(64 * blk + 32 * a, 32), 32)
                    own = pl.ds(pl.multiple_of(64 * blk + 32 * a + 16 * kappa, 16), 16)
                    l_re = pl.ds(pl.multiple_of(32 * blk + 16 * a, 16), 16)
                    l_im = pl.ds(pl.multiple_of(512 + 32 * blk + 16 * a, 16), 16)
                    for k in range(2):
                        comp = 2 * a + k
                        real = ref[at // 2, pl.ds(64 * comp + row, 32), :].astype(jnp.float32)
                        imag = ref[at // 2, pl.ds(64 * (4 + comp) + row, 32), :].astype(jnp.float32)
                        c_re = slice((4 * h + 2 * k) * LANES, (4 * h + 2 * k + 1) * LANES)
                        c_im = slice((4 * h + 2 * k + 1) * LANES, (4 * h + 2 * k + 2) * LANES)
                        g_ref[g_rows, c_re] = (real * cosine + imag * sine).astype(jnp.bfloat16)
                        g_ref[g_rows, c_im] = (imag * cosine - real * sine).astype(jnp.bfloat16)
                        x_re = g_ref[own, c_re]
                        x_im = g_ref[own, c_im]
                        l_ref[l_re, c_re] = x_re
                        l_ref[l_re, c_im] = x_im
                        l_ref[l_im, c_re] = x_im
                        l_ref[l_im, c_im] = -x_re
                return carry

            lax.fori_loop(0, 2 * count, step, 0)


def gram_slab(l_ref, g_ref, acc_ref, add):
    for tile in range(4):
        rows = (tile + 1) * 128
        cols = slice(256 * tile, 256 * tile + 256)
        for part in range(2):
            at = slice(512 * part, 512 * part + rows)
            got = lax.dot_general(
                l_ref[at, :], g_ref[cols, :], (((1,), (1,)), ((), ())),
                preferred_element_type=jnp.float32,
            )
            acc_ref[at, cols] = (acc_ref[at, cols] + got) if add else got


def near_kernel(slabs, scal_ref, kap_ref, uvw_ref, *refs):
    acc_ref, g_ref, l_ref = refs[-3:]
    for n in range(slabs):
        pieces = [[(refs[2 * n], 0)], [(refs[2 * n + 1], 0)]]
        field_slab(pieces, uvw_ref, scal_ref[0], kap_ref[0], g_ref, l_ref)
        gram_slab(l_ref, g_ref, acc_ref, n > 0)


def far_kernel(scal_ref, kap_ref, idx_ref, uvw_ref, a0, b0, a1, b1, near_ref, out_ref, acc_ref, g_ref, l_ref):
    pieces = [[(a0, 0), (b0, 4)], [(a1, 0), (b1, 4)]]
    field_slab(pieces, uvw_ref, scal_ref[0], kap_ref[0], g_ref, l_ref)
    gram_slab(l_ref, g_ref, acc_ref, False)
    low = lax.broadcasted_iota(jnp.int32, (16, LANES), 1) < 64
    for i in range(NBLK):
        for tile in range(i // 2, NBLK // 2):
            cols = slice(LANES * tile, LANES * tile + LANES)
            for part in range(2):
                top = 512 * part + 32 * i
                row0 = (acc_ref[top : top + 16, cols] + near_ref[top : top + 16, cols]) * SEND_SCALE
                row1 = (acc_ref[top + 16 : top + 32, cols] + near_ref[top + 16 : top + 32, cols]) * SEND_SCALE
                if i <= 2 * tile:
                    even = jnp.where(low, row0, pltpu.roll(row1, 64, 1))
                    out_ref[idx_ref[i * NBLK + 2 * tile] + PAIRS_DEV * part] = even.astype(out_ref.dtype)
                odd = jnp.where(low, pltpu.roll(row0, 64, 1), row1)
                out_ref[idx_ref[i * NBLK + 2 * tile + 1] + PAIRS_DEV * part] = odd.astype(out_ref.dtype)


def sum_kernel(got_ref, order_ref, out_ref, held_ref):
    total = got_ref[0].astype(jnp.float32)
    for n in range(1, got_ref.shape[0]):
        total = total + got_ref[n].astype(jnp.float32)
    total = total * (1.0 / SEND_SCALE)
    held_ref[...] = jnp.dot(
        total, order_ref[...], precision=lax.Precision.HIGHEST, preferred_element_type=jnp.float32
    )
    for st in range(16):
        out_ref[:, LANES * st : LANES * st + LANES] = held_ref[pl.ds(st, PAIRS_DEV, stride=16), :]


VMEM = pl.BlockSpec(memory_space=pltpu.VMEM)
SMEM = pl.BlockSpec(memory_space=pltpu.SMEM)
PARAMS = pltpu.CompilerParams(vmem_limit_bytes=56 * 1024 * 1024)
WORK = [pltpu.VMEM((KCOL, KCOL), jnp.bfloat16), pltpu.VMEM((KCOL, KCOL), jnp.bfloat16)]
SEND = jnp.bfloat16


def src_step(dz, dcore):
    return [
        (z * 4 + xh * 2 + core, ((z + dz) % 4) * 4 + xh * 2 + (core ^ dcore))
        for z in range(4) for xh in range(2) for core in range(2)
    ]


PLANES = [
    [stn * 16 + z * 4 + xh * 2 + core for stn in range(STN) for xh in range(2)]
    for z in range(4) for core in range(2)
]


def split3(x):
    first = lax.reduce_precision(x, 8, 7)
    second = lax.reduce_precision(x - first, 8, 7)
    third = x - first - second
    return [v.astype(jnp.bfloat16) for v in (first, second, third)]


def body(beam_jones, source_lm, source_flux, live_counts, station_uvw, chan_scale, block_pairs):
    src = lax.axis_index("src")
    plane = src // 4
    kappa = (src % 2).astype(jnp.int32).reshape(1)
    slots = beam_jones.shape[2]
    live = (jnp.arange(slots, dtype=jnp.int32) < live_counts[0]).astype(jnp.float32)
    amp = jnp.sqrt(source_flux * live / math.sqrt(slots * 16))
    dir_l, dir_m = source_lm[0], source_lm[1]
    depth = jnp.sqrt(1.0 - dir_l * dir_l - dir_m * dir_m) - 1.0
    extra = []
    for row in (dir_l, dir_m, depth, amp):
        extra += [v.reshape(STN, LANES) for v in split3(row)]
    pairs = jnp.pad(block_pairs.T.astype(jnp.bfloat16), ((0, 0), (0, LANES - PAIRS_DEV)))
    extra += [jnp.broadcast_to(pairs[n][None], (STN, LANES)) for n in range(2)]
    extra += [jnp.zeros((STN, LANES), jnp.bfloat16)] * (EXTRA - len(extra))
    extra = jnp.stack(extra, axis=1)
    pieces = jnp.transpose(beam_jones.reshape(JROWS, STN, LANES), (1, 0, 2))
    message = jnp.concatenate([pieces, extra], axis=1)

    own = lax.all_to_all(message, "stn", 0, 0, tiled=True)

    def move(x, dz, dcore=0):
        return lax.ppermute(x, "src", src_step(dz, dcore))

    below = move(own, 1)
    above = move(own, -1)
    far_a = move(below[:4], 1)
    far_b = move(above[4:], -1)
    near = []
    for slab in (own, below, above):
        near += [slab, move(slab, 0, 1)]
    far = [far_a, far_b, move(far_a, 0, 1), move(far_b, 0, 1)]

    listed = own[:, JROWS + 12 : JROWS + 14, :PAIRS_DEV].astype(jnp.int32)
    number = jnp.arange(STN * PAIRS_DEV, dtype=jnp.int32)
    place = (number // PAIRS_DEV) * (2 * PAIRS_DEV) + number % PAIRS_DEV
    key = (listed[:, 0] * NBLK + listed[:, 1]).reshape(1, -1)
    hit = key == jnp.arange(NBLK * NBLK, dtype=jnp.int32)[:, None]
    index = jnp.sum(jnp.where(hit, place[None], 0), axis=1)

    scale = (2.0 * math.pi * chan_scale)[plane].reshape(1)
    uvw = jnp.broadcast_to(station_uvw[:, :, None], (3, station_uvw.shape[1], LANES))

    partial = pl.pallas_call(
        functools.partial(near_kernel, 3),
        out_shape=jax.ShapeDtypeStruct((KCOL, KCOL), jnp.float32),
        in_specs=[SMEM, SMEM, VMEM] + [VMEM] * 6,
        out_specs=VMEM,
        scratch_shapes=WORK,
        compiler_params=PARAMS,
        cost_estimate=pl.CostEstimate(flops=4_000_000_000, bytes_accessed=11_000_000, transcendentals=0),
    )(scale, kappa, uvw, *near)
    send = pl.pallas_call(
        far_kernel,
        out_shape=jax.ShapeDtypeStruct((STN * 2 * PAIRS_DEV, 16, LANES), SEND),
        in_specs=[SMEM, SMEM, SMEM, VMEM] + [VMEM] * 5,
        out_specs=VMEM,
        scratch_shapes=[pltpu.VMEM((KCOL, KCOL), jnp.float32)] + WORK,
        compiler_params=PARAMS,
        cost_estimate=pl.CostEstimate(flops=1_400_000_000, bytes_accessed=8_000_000, transcendentals=0),
    )(scale, kappa, index, uvw, *far, partial)

    send = send.reshape(STN * 2, PAIRS_DEV * 16, LANES)
    got = lax.all_to_all(send, ("stn", "src"), 0, 0, axis_index_groups=PLANES, tiled=True)

    lane = np.arange(LANES)
    order = np.zeros((LANES, LANES), np.float32)
    order[lane, (lane // 64) * 64 + (lane % 32) * 2 + (lane // 32) % 2] = 1.0
    return pl.pallas_call(
        sum_kernel,
        out_shape=jax.ShapeDtypeStruct((PAIRS_DEV, 2048), jnp.float32),
        in_specs=[VMEM, VMEM],
        out_specs=VMEM,
        scratch_shapes=[pltpu.VMEM((PAIRS_DEV * 16, LANES), jnp.float32)],
        compiler_params=PARAMS,
    )(got, jnp.asarray(order))


def solution(mesh):
    placed = (P(None, "stn", "src"), P(None, "src"), P("src"), P("src"), P(), P(), P("stn", None))
    return jax.shard_map(
        body, mesh=mesh, in_specs=placed, out_specs=P("stn", "src"), check_vma=False
    )
```

```python
import functools
import math

import jax
import jax.numpy as jnp
import numpy as np
from jax import lax
from jax.experimental import pallas as pl
from jax.experimental.pallas import tpu as pltpu
from jax.sharding import PartitionSpec as P

NBLK = 16
STN = 8
PAIRS_DEV = 17
LANES = 128
JROWS = 256
EXTRA = 16
ROWS = JROWS + EXTRA
OUT_ROWS = PAIRS_DEV * 16
KCOL = 1024

TWO_PI_HI = 6.28125
TWO_PI_LO = 2.0 * math.pi - 6.28125
def _fit(fun, power, terms):
    x = np.cos(np.pi * (np.arange(4000) + 0.5) / 4000) * (math.pi * 1.001)
    cols = np.stack([x ** (2 * n + power) for n in range(terms)], 1)
    scale = np.abs(cols).max(0)
    sol, *_ = np.linalg.lstsq(cols / scale, fun(x), rcond=None)
    return [float(v) for v in sol / scale]


SIN_TERMS = _fit(np.sin, 1, 7)
COS_TERMS = _fit(np.cos, 0, 8)


def horner(square, terms):
    total = jnp.full_like(square, terms[-1])
    for term in terms[-2::-1]:
        total = total * square + term
    return total


def three(rows, at):
    return (rows[at : at + 1] + rows[at + 1 : at + 2]) + rows[at + 2 : at + 3]


def split3(x):
    first = x.astype(jnp.bfloat16).astype(jnp.float32)
    second = (x - first).astype(jnp.bfloat16).astype(jnp.float32)
    return [first, second, x - first - second]


def prep_kernel(live_ref, lm_hbm, flux_hbm, pairs_hbm, jones_hbm, even_ref, odd_ref, *refs):
    lm_ref, flux_ref, pairs_ref, jones_ref, info_ref, sems = refs
    copies = [
        pltpu.make_async_copy(src, dst, sems.at[n])
        for n, (src, dst) in enumerate(
            ((jones_hbm, jones_ref), (lm_hbm, lm_ref), (flux_hbm, flux_ref), (pairs_hbm, pairs_ref))
        )
    ]
    for copy in copies:
        copy.start()
    for copy in copies[1:]:
        copy.wait()
    slots = jones_ref.shape[2]
    dir_l, dir_m = lm_ref[0:1, :], lm_ref[1:2, :]
    live = (lax.broadcasted_iota(jnp.int32, (1, slots), 1) < live_ref[0]).astype(jnp.float32)
    amp = jnp.sqrt(flux_ref[...] * live * (1.0 / math.sqrt(slots * 16)))
    depth = jnp.sqrt(1.0 - dir_l * dir_l - dir_m * dir_m) - 1.0
    info_ref[...] = jnp.zeros_like(info_ref)
    for n, row in enumerate((dir_l, dir_m, depth, amp)):
        for t, term in enumerate(split3(row)):
            info_ref[3 * n + t : 3 * n + t + 1, :] = term
    for d in range(STN):
        info_ref[12:14, LANES * d : LANES * d + PAIRS_DEV] = pairs_ref[...].astype(jnp.float32)
    copies[0].wait()
    for d in range(STN):
        cols = slice(LANES * d, LANES * d + LANES)
        for comp in range(8):
            even_ref[d, 32 * comp : 32 * comp + 32, :] = jones_ref[comp, 0:32, cols]
            odd_ref[d, 32 * comp : 32 * comp + 32, :] = jones_ref[comp, 32:64, cols]
        even_ref[d, JROWS:ROWS, :] = info_ref[:, cols].astype(jnp.bfloat16)


def field_slab(pieces, uvw_ref, scale, kappa, g_ref, l_ref):
    for h, halves in enumerate(pieces):
        info = halves[0][0, JROWS:ROWS, :].astype(jnp.float32)
        dir_l, dir_m, depth, amp = (three(info, 3 * n) for n in range(4))

        def step(stn, carry):
            for odd, ref in enumerate(halves):
                blk = 2 * stn + odd
                here = pl.ds(pl.multiple_of(32 * blk, 32), 32)
                geometry = (
                    uvw_ref[0, here, :] * dir_l + uvw_ref[1, here, :] * dir_m
                ) + uvw_ref[2, here, :] * depth
                phase = scale * geometry
                turns = jnp.round(phase * (0.5 / math.pi))
                angle = (phase - turns * TWO_PI_HI) - turns * TWO_PI_LO
                square = angle * angle
                sine = horner(square, SIN_TERMS) * (angle * amp)
                cosine = horner(square, COS_TERMS) * amp
                for a in range(2):
                    g_rows = pl.ds(pl.multiple_of(64 * blk + 32 * a, 32), 32)
                    own = pl.ds(pl.multiple_of(64 * blk + 32 * a + 16 * kappa, 16), 16)
                    l_re = pl.ds(pl.multiple_of(32 * blk + 16 * a, 16), 16)
                    l_im = pl.ds(pl.multiple_of(512 + 32 * blk + 16 * a, 16), 16)
                    for k in range(2):
                        comp = 2 * a + k
                        real = ref[stn, 32 * comp : 32 * comp + 32, :].astype(jnp.float32)
                        imag = ref[stn, 128 + 32 * comp : 160 + 32 * comp, :].astype(jnp.float32)
                        c_re = slice((4 * h + 2 * k) * LANES, (4 * h + 2 * k + 1) * LANES)
                        c_im = slice((4 * h + 2 * k + 1) * LANES, (4 * h + 2 * k + 2) * LANES)
                        g_ref[g_rows, c_re] = (real * cosine + imag * sine).astype(jnp.bfloat16)
                        g_ref[g_rows, c_im] = (imag * cosine - real * sine).astype(jnp.bfloat16)
                        x_re = g_ref[own, c_re]
                        x_im = g_ref[own, c_im]
                        l_ref[l_re, c_re] = x_re
                        l_ref[l_re, c_im] = x_im
                        l_ref[l_im, c_re] = x_im
                        l_ref[l_im, c_im] = -x_re
            return carry

        lax.fori_loop(0, STN, step, 0)


def gram_slab(l_ref, g_ref, before_ref, acc_ref):
    for tile in range(4):
        rows = (tile + 1) * 128
        cols = slice(256 * tile, 256 * tile + 256)
        for part in range(2):
            at = slice(512 * part, 512 * part + rows)
            got = lax.dot_general(
                l_ref[at, :], g_ref[cols, :], (((1,), (1,)), ((), ())),
                preferred_element_type=jnp.float32,
            )
            acc_ref[at, cols] = got if before_ref is None else before_ref[at, cols] + got


def pack_pairs(acc_ref, idx_ref, out_ref):
    low = lax.broadcasted_iota(jnp.int32, (16, LANES), 1) < 64
    for i in range(NBLK):
        for tile in range(i // 2, NBLK // 2):
            cols = slice(LANES * tile, LANES * tile + LANES)
            for part in range(2):
                top = 512 * part + 32 * i
                row0 = acc_ref[top : top + 16, cols]
                row1 = acc_ref[top + 16 : top + 32, cols]
                at = (part * NBLK + i) * NBLK + 2 * tile
                if i <= 2 * tile:
                    even = jnp.where(low, row0, pltpu.roll(row1, 64, 1))
                    out_ref[idx_ref[at]] = even.astype(out_ref.dtype)
                odd = jnp.where(low, pltpu.roll(row0, 64, 1), row1)
                out_ref[idx_ref[at + 1]] = odd.astype(out_ref.dtype)


def own_near_kernel(scal_ref, int_ref, uvw_ref, a0, b0, a1, b1, acc_ref, g_ref, l_ref):
    field_slab([(a0, b0), (a1, b1)], uvw_ref, scal_ref[0], int_ref[0], g_ref, l_ref)
    gram_slab(l_ref, g_ref, None, acc_ref)


def own_far_kernel(scal_ref, int_ref, idx_ref, uvw_ref, a0, b0, a1, b1, out_ref, acc_ref, g_ref, l_ref):
    field_slab([(a0, b0), (a1, b1)], uvw_ref, scal_ref[1], int_ref[0], g_ref, l_ref)
    gram_slab(l_ref, g_ref, None, acc_ref)
    pack_pairs(acc_ref, idx_ref, out_ref)


def side_own_kernel(scal_ref, int_ref, uvw_ref, a0, b0, a1, b1, before_hbm, acc_ref, before_ref, g_ref, l_ref, sem):
    copy = pltpu.make_async_copy(before_hbm, before_ref, sem)
    copy.start()
    field_slab([(a0, b0), (a1, b1)], uvw_ref, scal_ref[0], int_ref[0], g_ref, l_ref)
    copy.wait()
    gram_slab(l_ref, g_ref, before_ref, acc_ref)


def side_other_kernel(scal_ref, int_ref, idx_ref, uvw_ref, a0, b0, a1, b1, before_hbm, out_ref,
                      acc_ref, before_ref, g_ref, l_ref, sem):
    copy = pltpu.make_async_copy(before_hbm, before_ref, sem)
    copy.start()
    field_slab([(a0, b0), (a1, b1)], uvw_ref, scal_ref[0], int_ref[0], g_ref, l_ref)
    copy.wait()
    gram_slab(l_ref, g_ref, before_ref, acc_ref)
    pack_pairs(acc_ref, idx_ref, out_ref)


def far_sum_kernel(got_ref, out_ref):
    total = got_ref[0].astype(jnp.float32)
    for n in range(1, got_ref.shape[0]):
        total = total + got_ref[n].astype(jnp.float32)
    out_ref[...] = total


def sum_kernel(got_ref, far_ref, order_ref, out_ref, held_ref):
    total = far_ref[...]
    for n in range(got_ref.shape[0]):
        total = total + got_ref[n].astype(jnp.float32)
    held_ref[...] = jnp.dot(
        total, order_ref[...], precision=lax.Precision.HIGHEST, preferred_element_type=jnp.float32
    )
    for st in range(16):
        out_ref[:, LANES * st : LANES * st + LANES] = held_ref[pl.ds(st, PAIRS_DEV, stride=16), :]


VMEM = pl.BlockSpec(memory_space=pltpu.VMEM)
SMEM = pl.BlockSpec(memory_space=pltpu.SMEM)
PARAMS = pltpu.CompilerParams(vmem_limit_bytes=24 * 1024 * 1024)
ANY = pl.BlockSpec(memory_space=pl.ANY)
WORK = [pltpu.VMEM((KCOL, KCOL), jnp.bfloat16), pltpu.VMEM((KCOL, KCOL), jnp.bfloat16)]
SEND = jnp.bfloat16


def coords():
    return [(xl, y, z, xh, core) for xl in range(2) for y in range(4) for z in range(4) for xh in range(2) for core in range(2)]


def place_of(xl, y, z, xh, core):
    return (xl * 4 + y % 4) * 16 + (z % 4) * 4 + xh * 2 + core


def move(x, dx=0, dy=0, dz=0, dcore=0):
    perm = []
    for xl, y, z, xh, core in coords():
        x_to = (2 * xh + xl + dx) % 4
        perm.append((place_of(xl, y, z, xh, core), place_of(x_to % 2, y + dy, z + dz, x_to // 2, core ^ dcore)))
    return lax.ppermute(x, ("stn", "src"), perm)


PLANES = [
    [stn * 16 + z * 4 + xh * 2 + core for stn in range(STN) for xh in range(2)]
    for z in range(4) for core in range(2)
]


def body(beam_jones, source_lm, source_flux, live_counts, station_uvw, chan_scale, block_pairs):
    src, stn = lax.axis_index("src"), lax.axis_index("stn")
    plane = src // 4
    ints = (src % 2).reshape(1).astype(jnp.int32)
    even, odd = pl.pallas_call(
        prep_kernel,
        out_shape=[jax.ShapeDtypeStruct((STN, n, LANES), jnp.bfloat16) for n in (ROWS, JROWS)],
        in_specs=[SMEM] + [pl.BlockSpec(memory_space=pl.ANY)] * 4,
        out_specs=[VMEM, VMEM],
        scratch_shapes=[
            pltpu.VMEM((2, STN * LANES), jnp.float32),
            pltpu.VMEM((1, STN * LANES), jnp.float32),
            pltpu.VMEM((2, PAIRS_DEV), jnp.int32),
            pltpu.VMEM((8, 64, STN * LANES), jnp.bfloat16),
            pltpu.VMEM((EXTRA, STN * LANES), jnp.float32),
            pltpu.SemaphoreType.DMA((4,)),
        ],
        compiler_params=pltpu.CompilerParams(vmem_limit_bytes=62 * 1024 * 1024),
    )(live_counts, source_lm, source_flux.reshape(1, -1), block_pairs.T, beam_jones)

    first = lax.all_to_all(even, "stn", 0, 0, tiled=True)
    first, odd = lax.optimization_barrier((first, odd))
    own = [first, lax.all_to_all(odd, "stn", 0, 0, tiled=True)]
    below_a, above_a = move(own[0], dz=1), move(own[0], dz=-1)
    own += [move(x, dcore=1) for x in own]

    listed = own[0][:, JROWS + 12 : JROWS + 14, :PAIRS_DEV].astype(jnp.int32)
    holder = jnp.repeat(jnp.arange(STN, dtype=jnp.int32), PAIRS_DEV)
    slot = jnp.tile(jnp.arange(PAIRS_DEV, dtype=jnp.int32), STN)
    key = (listed[:, 0] * NBLK + listed[:, 1]).reshape(1, -1)
    hit = key == jnp.arange(NBLK * NBLK, dtype=jnp.int32)[:, None]
    part = jnp.arange(2, dtype=jnp.int32)[:, None]
    place = (holder * 2 + part) * PAIRS_DEV + slot
    index = jnp.sum(jnp.where(hit[None], place[:, None, :], 0), axis=2).reshape(-1)

    scale = (2.0 * math.pi * chan_scale)[jnp.stack([plane, (plane + 2) % 4])]
    uvw = jnp.broadcast_to(station_uvw[:, :, None], (3, station_uvw.shape[1], LANES))

    def work(shape, *more, copied=False):
        scratch = [*more, *WORK] + ([pltpu.SemaphoreType.DMA(())] if copied else [])
        return dict(out_specs=VMEM, scratch_shapes=scratch, compiler_params=PARAMS, out_shape=shape)

    total = jax.ShapeDtypeStruct((KCOL, KCOL), jnp.float32)

    packed = jax.ShapeDtypeStruct((STN * 2 * PAIRS_DEV, 16, LANES), SEND)
    square = pltpu.VMEM((KCOL, KCOL), jnp.float32)
    far = pl.pallas_call(
        own_far_kernel, in_specs=[SMEM] * 3 + [VMEM] * 5, **work(packed, square)
    )(scale, ints, index, uvw, *own)
    below_a, above_a, later, far, own_again = lax.optimization_barrier((below_a, above_a, own[1], far, own[0]))
    below, above = [below_a, move(later, dz=1)], [above_a, move(later, dz=-1)]
    far = lax.all_to_all(
        far.reshape(STN * 2, OUT_ROWS, LANES), ("stn", "src"), 0, 0, axis_index_groups=PLANES, tiled=True
    )
    near = pl.pallas_call(
        own_near_kernel, in_specs=[SMEM] * 2 + [VMEM] * 5, **work(total)
    )(scale, ints, uvw, own_again, *own[1:])

    near, below[1], above[1] = lax.optimization_barrier((near, below[1], above[1]))
    others = [move(x, dcore=1) for x in (*below, *above)]
    near = pl.pallas_call(
        side_own_kernel, in_specs=[SMEM] * 2 + [VMEM] * 5 + [ANY], **work(total, square, copied=True),
    )(scale, ints, uvw, *below, *above, near)
    near, *others = lax.optimization_barrier((near, *others))
    send = pl.pallas_call(
        side_other_kernel, in_specs=[SMEM] * 3 + [VMEM] * 5 + [ANY],
        **work(packed, square, square, copied=True),
    )(scale, ints, index, uvw, *others, near)

    send, far = lax.optimization_barrier((send, far))
    far_sum = pl.pallas_call(
        far_sum_kernel,
        out_shape=jax.ShapeDtypeStruct((OUT_ROWS, LANES), jnp.float32),
        in_specs=[VMEM], out_specs=VMEM, compiler_params=PARAMS,
    )(far)
    far_got = move(far_sum, dz=2)

    send = send.reshape(STN * 2, PAIRS_DEV * 16, LANES)
    got = lax.all_to_all(send, ("stn", "src"), 0, 0, axis_index_groups=PLANES, tiled=True)

    lane = np.arange(LANES)
    order = np.zeros((LANES, LANES), np.float32)
    order[lane, (lane // 64) * 64 + (lane % 32) * 2 + (lane // 32) % 2] = 1.0
    return pl.pallas_call(
        sum_kernel,
        out_shape=jax.ShapeDtypeStruct((PAIRS_DEV, 2048), jnp.float32),
        in_specs=[VMEM] * 3,
        out_specs=VMEM,
        scratch_shapes=[pltpu.VMEM((PAIRS_DEV * 16, LANES), jnp.float32)],
        compiler_params=PARAMS,
    )(got, far_got, jnp.asarray(order))


def solution(mesh):
    placed = (P(None, "stn", "src"), P(None, "src"), P("src"), P("src"), P(), P(), P("stn", None))
    return jax.shard_map(
        body, mesh=mesh, in_specs=placed, out_specs=P("stn", "src"), check_vma=False
    )
```

```python
import functools
import math

import jax
import jax.numpy as jnp
import numpy as np
from jax import lax
from jax.experimental import pallas as pl
from jax.experimental.pallas import tpu as pltpu
from jax.sharding import PartitionSpec as P

NBLK = 16
STN = 8
PAIRS_DEV = 17
LANES = 128
JROWS = 512
EXTRA = 16
ROWS = JROWS + EXTRA
OUT_ROWS = PAIRS_DEV * 16
KCOL = 512
ACC = (2560, 256)

TWO_PI_HI = 6.28125
TWO_PI_LO = 2.0 * math.pi - 6.28125
def _fit(fun, power, terms):
    x = np.cos(np.pi * (np.arange(4000) + 0.5) / 4000) * (math.pi * 1.001)
    cols = np.stack([x ** (2 * n + power) for n in range(terms)], 1)
    scale = np.abs(cols).max(0)
    sol, *_ = np.linalg.lstsq(cols / scale, fun(x), rcond=None)
    return [float(v) for v in sol / scale]


SIN_TERMS = _fit(np.sin, 1, 7)
COS_TERMS = _fit(np.cos, 0, 8)


def horner(square, terms):
    total = jnp.full_like(square, terms[-1])
    for term in terms[-2::-1]:
        total = total * square + term
    return total


def three(rows, at):
    return (rows[at : at + 1] + rows[at + 1 : at + 2]) + rows[at + 2 : at + 3]


def split3(x):
    first = x.astype(jnp.bfloat16).astype(jnp.float32)
    second = (x - first).astype(jnp.bfloat16).astype(jnp.float32)
    return [first, second, x - first - second]


def prep_kernel(live_ref, lm_hbm, flux_hbm, pairs_hbm, jones_hbm, out_ref, *refs):
    lm_ref, flux_ref, pairs_ref, jones_ref, info_ref, sems = refs
    copies = [
        pltpu.make_async_copy(src, dst, sems.at[n])
        for n, (src, dst) in enumerate(
            ((jones_hbm, jones_ref), (lm_hbm, lm_ref), (flux_hbm, flux_ref), (pairs_hbm, pairs_ref))
        )
    ]
    for copy in copies:
        copy.start()
    for copy in copies[1:]:
        copy.wait()
    slots = jones_ref.shape[2]
    dir_l, dir_m = lm_ref[0:1, :], lm_ref[1:2, :]
    live = (lax.broadcasted_iota(jnp.int32, (1, slots), 1) < live_ref[0]).astype(jnp.float32)
    amp = jnp.sqrt(flux_ref[...] * live * (1.0 / math.sqrt(slots * 16)))
    depth = jnp.sqrt(1.0 - dir_l * dir_l - dir_m * dir_m) - 1.0
    info_ref[...] = jnp.zeros_like(info_ref)
    for n, row in enumerate((dir_l, dir_m, depth, amp)):
        for t, term in enumerate(split3(row)):
            info_ref[3 * n + t : 3 * n + t + 1, :] = term
    for d in range(STN):
        info_ref[12:14, LANES * d : LANES * d + PAIRS_DEV] = pairs_ref[...].astype(jnp.float32)
    copies[0].wait()
    src = lax.axis_index("src")
    first = 2 * (src // 4) + src % 2
    for d in range(STN):
        cols = pl.ds(pl.multiple_of((d + first) % STN * LANES, LANES), LANES)
        for comp in range(8):
            out_ref[d, 64 * comp : 64 * comp + 64, :] = jones_ref[comp, :, cols]
        out_ref[d, JROWS:ROWS, :] = info_ref[:, cols].astype(jnp.bfloat16)


def acc_at(tile, part):
    return 256 * (tile * (tile + 1) // 2) + 128 * (tile + 1) * part


def gram_piece(step, l_ref, g_ref, before_ref, acc_ref):
    tile, part = 3 - step // 2, step % 2
    rows = 128 * (tile + 1)
    at = acc_at(tile, part)
    got = lax.dot_general(
        l_ref[512 * part : 512 * part + rows, :], g_ref[256 * tile : 256 * tile + 256, :],
        (((1,), (1,)), ((), ())), preferred_element_type=jnp.float32,
    )
    acc_ref[at : at + rows, :] = got if before_ref is None else before_ref[at : at + rows, :] + got


def field_piece(stn, held, uvw_ref, scale, kappa, g_ref, l_ref):
    ref, at = (held[0], stn) if len(held) == 1 else (held[stn // 4], stn % 4)
    info = ref[0, JROWS:ROWS, :].astype(jnp.float32)
    dir_l, dir_m, depth, amp = (three(info, 3 * n) for n in range(4))
    for odd in range(2):
        blk = 2 * stn + odd
        here = slice(32 * blk, 32 * blk + 32)
        geometry = (uvw_ref[0, here, :] * dir_l + uvw_ref[1, here, :] * dir_m) + uvw_ref[2, here, :] * depth
        phase = scale * geometry
        turns = jnp.round(phase * (0.5 / math.pi))
        angle = (phase - turns * TWO_PI_HI) - turns * TWO_PI_LO
        square = angle * angle
        sine = horner(square, SIN_TERMS) * (angle * amp)
        cosine = horner(square, COS_TERMS) * amp
        for a in range(2):
            g_rows = slice(64 * blk + 32 * a, 64 * blk + 32 * a + 32)
            own = pl.ds(pl.multiple_of(64 * blk + 32 * a + 16 * kappa, 16), 16)
            l_re = slice(32 * blk + 16 * a, 32 * blk + 16 * a + 16)
            l_im = slice(512 + 32 * blk + 16 * a, 512 + 32 * blk + 16 * a + 16)
            for k in range(2):
                row = 64 * (2 * a + k) + 32 * odd
                real = ref[at, row : row + 32, :].astype(jnp.float32)
                imag = ref[at, 256 + row : 288 + row, :].astype(jnp.float32)
                c_re = slice(2 * k * LANES, (2 * k + 1) * LANES)
                c_im = slice((2 * k + 1) * LANES, (2 * k + 2) * LANES)
                g_ref[g_rows, c_re] = (real * cosine + imag * sine).astype(jnp.bfloat16)
                g_ref[g_rows, c_im] = (imag * cosine - real * sine).astype(jnp.bfloat16)
                x_re = g_ref[own, c_re]
                x_im = g_ref[own, c_im]
                l_ref[l_re, c_re] = x_re
                l_ref[l_re, c_im] = x_im
                l_ref[l_im, c_re] = x_im
                l_ref[l_im, c_im] = -x_re


def pack_pairs(acc_ref, idx_ref, out_ref):
    low = lax.broadcasted_iota(jnp.int32, (16, LANES), 1) < 64
    for i in range(NBLK):
        for tile in range(i // 2, NBLK // 2):
            cols = slice(LANES * (tile % 2), LANES * (tile % 2) + LANES)
            for part in range(2):
                top = acc_at(tile // 2, part) + 32 * i
                row0 = acc_ref[top : top + 16, cols]
                row1 = acc_ref[top + 16 : top + 32, cols]
                at = (part * NBLK + i) * NBLK + 2 * tile
                if i <= 2 * tile:
                    even = jnp.where(low, row0, pltpu.roll(row1, 64, 1))
                    out_ref[idx_ref[at]] = even.astype(out_ref.dtype)
                odd = jnp.where(low, pltpu.roll(row0, 64, 1), row1)
                out_ref[idx_ref[at + 1]] = odd.astype(out_ref.dtype)


def slab_kernel(chan, packs, chained, counts, *refs):
    scal_ref, int_ref, *refs = refs
    idx_ref = refs.pop(0) if packs else None
    uvw_ref, *refs = refs
    sets, source_refs = len(counts), []
    for count in counts:
        source_refs.append(refs[:count])
        refs = refs[count:]
    before_ref = refs.pop(0) if chained else None
    out_refs, refs = (refs[:4], refs[4:]) if packs else (refs[:1], refs[1:])
    acc_ref, held_ref, sems = refs[4:] if packs else (out_refs[0], None, None)
    work = (refs[0:2], refs[2:4])
    scale, kappa = scal_ref[chan], int_ref[0]
    for n in range(sets + 1):
        for step in range(STN):
            if n < sets:
                field_piece(step, source_refs[n], uvw_ref, scale, kappa, *work[n % 2])
            if n > 0:
                g_ref, l_ref = work[(n - 1) % 2]
                gram_piece(step, l_ref, g_ref, acc_ref if n > 1 else before_ref, acc_ref)
    if packs:
        pack_pairs(acc_ref, idx_ref, held_ref)
        each = 4 * PAIRS_DEV
        copies = [
            pltpu.make_async_copy(held_ref.at[each * n : each * n + each], out_ref, sems.at[n])
            for n, out_ref in enumerate(out_refs)
        ]
        for copy in copies:
            copy.start()
        for copy in copies:
            copy.wait()


def add_far_kernel(one, two, three, four, real_ref, imag_ref):
    total = one[...].astype(jnp.float32)
    for ref in (two, three, four):
        total = total + ref[...].astype(jnp.float32)
    real_ref[...] = total[: 2 * PAIRS_DEV]
    imag_ref[...] = total[2 * PAIRS_DEV :].astype(imag_ref.dtype)


def add_near_kernel(int_ref, one, two, three, four, real_ref, imag_ref, *outs):
    for n, out_ref in enumerate(outs):
        rows = slice(PAIRS_DEV * n, PAIRS_DEV * n + PAIRS_DEV)
        total = one[rows].astype(jnp.float32)
        for ref in (two, three, four):
            total = total + ref[rows].astype(jnp.float32)
        x_to = (int_ref[1] + n) % 4
        there = pl.ds(x_to % 2 * PAIRS_DEV, PAIRS_DEV)
        far = jnp.where(x_to < 2, real_ref[there], imag_ref[there].astype(jnp.float32))
        out_ref[...] = (total + far).reshape(out_ref.shape)


def sum_kernel(*refs):
    shares, (order_ref, out_ref, held_ref) = refs[:-3], refs[-3:]
    total = shares[0][...]
    for ref in shares[1:]:
        total = total + ref[...]
    held_ref[...] = jnp.dot(
        total, order_ref[...], precision=lax.Precision.HIGHEST, preferred_element_type=jnp.float32
    )
    for st in range(16):
        out_ref[:, LANES * st : LANES * st + LANES] = held_ref[pl.ds(st, PAIRS_DEV, stride=16), :]


VMEM = pl.BlockSpec(memory_space=pltpu.VMEM)
SMEM = pl.BlockSpec(memory_space=pltpu.SMEM)
PARAMS = pltpu.CompilerParams(vmem_limit_bytes=14 * 1024 * 1024)
ALONE = pltpu.CompilerParams(vmem_limit_bytes=62 * 1024 * 1024)
WORK = [pltpu.VMEM((1024, KCOL), jnp.bfloat16)] * 4
SEND = jnp.bfloat16


def coords():
    return [(xl, y, z, xh, core) for xl in range(2) for y in range(4) for z in range(4) for xh in range(2) for core in range(2)]


def place_of(xl, y, z, xh, core):
    return (xl * 4 + y % 4) * 16 + (z % 4) * 4 + xh * 2 + core


def move(x, dx=0, dy=0, dz=0, dcore=0, apart=0):
    perm = []
    for xl, y, z, xh, core in coords():
        x_to = (2 * xh + xl + dx) % 4
        z_to = z + dz + (apart if core == 0 else -apart)
        perm.append((place_of(xl, y, z, xh, core), place_of(x_to % 2, y + dy, z_to, x_to // 2, core ^ dcore)))
    return lax.ppermute(x, ("stn", "src"), perm)


def body(beam_jones, source_lm, source_flux, live_counts, station_uvw, chan_scale, block_pairs):
    src, stn = lax.axis_index("src"), lax.axis_index("stn")
    plane = src // 4
    x_own, y_own = 2 * ((src // 2) % 2) + stn // 4, stn % 4
    ints = jnp.stack([src % 2, x_own]).astype(jnp.int32)
    message = pl.pallas_call(
        prep_kernel,
        out_shape=jax.ShapeDtypeStruct((STN, ROWS, LANES), jnp.bfloat16),
        in_specs=[SMEM] + [pl.BlockSpec(memory_space=pl.ANY)] * 4,
        out_specs=VMEM,
        scratch_shapes=[
            pltpu.VMEM((2, STN * LANES), jnp.float32),
            pltpu.VMEM((1, STN * LANES), jnp.float32),
            pltpu.VMEM((2, PAIRS_DEV), jnp.int32),
            pltpu.VMEM((8, 64, STN * LANES), jnp.bfloat16),
            pltpu.VMEM((EXTRA, STN * LANES), jnp.float32),
            pltpu.SemaphoreType.DMA((4,)),
        ],
        compiler_params=ALONE,
    )(live_counts, source_lm, source_flux.reshape(1, -1), block_pairs.T, beam_jones)

    own = lax.all_to_all(message, "stn", 0, 0, tiled=True)
    got = [move(own[:4], apart=1), move(own[4:], apart=1)]
    other = move(own, dcore=1)

    listed = other[:, JROWS + 12 : JROWS + 14, :PAIRS_DEV].astype(jnp.int32)
    holder = jnp.repeat(jnp.arange(STN, dtype=jnp.int32), PAIRS_DEV)
    slot = jnp.tile(jnp.arange(PAIRS_DEV, dtype=jnp.int32), STN)
    key = (listed[:, 0] * NBLK + listed[:, 1]).reshape(1, -1)
    hit = key == jnp.arange(NBLK * NBLK, dtype=jnp.int32)[:, None]
    part = jnp.arange(2, dtype=jnp.int32)[:, None]
    dy, dx = (holder % 4 - y_own) % 4, (2 * part + holder // 4 - x_own) % 4
    place = jnp.stack([dy * 4 + dx, dy * 4 + 2 * part + holder // 4]) * PAIRS_DEV + slot
    index = jnp.sum(jnp.where(hit[None, None], place[:, :, None, :], 0), axis=3).reshape(2, -1)

    scale = (2.0 * math.pi * chan_scale)[jnp.stack([plane, (plane + 2) % 4])]
    uvw = jnp.broadcast_to(station_uvw[:, :, None], (3, station_uvw.shape[1], LANES))

    square = jax.ShapeDtypeStruct(ACC, jnp.float32)
    packed = [jax.ShapeDtypeStruct((4 * PAIRS_DEV, 16, LANES), SEND)] * 4

    def slab(chan, packs, sources, before=None):
        chained = before is not None
        flat = [x for held in sources for x in held]
        return pl.pallas_call(
            functools.partial(slab_kernel, chan, packs, chained, [len(x) for x in sources]),
            out_shape=packed if packs else square,
            in_specs=[SMEM] * (3 if packs else 2) + [VMEM] * (1 + len(flat) + chained),
            out_specs=[pl.BlockSpec(memory_space=pl.ANY)] * 4 if packs else VMEM,
            scratch_shapes=WORK + ([
                pltpu.VMEM(ACC, jnp.float32), pltpu.VMEM((16 * PAIRS_DEV, 16, LANES), SEND), pltpu.SemaphoreType.DMA((4,))
            ] if packs else []),
            input_output_aliases={3 + len(flat): 0} if chained and not packs else {},
            compiler_params=PARAMS,
        )(scale, ints, *([index[chan]] if packs else []), uvw, *flat, *([before] if chained else []))

    def along_y(shares):
        return [shares[0]] + [move(shares[n], dy=n) for n in (1, 2, 3)]

    far = slab(1, False, [[own], [other]])
    near = slab(0, False, [[own], [other]])
    near, far, *got = lax.optimization_barrier((near, far, *got))
    other = [move(x, dcore=1) for x in got]
    far = slab(1, False, [got], far)
    far, *other = lax.optimization_barrier((far, *other))
    far = slab(1, True, [other], far)
    near, *far = lax.optimization_barrier((near, *far))
    near = slab(0, True, [got, other], near)
    small = jax.ShapeDtypeStruct((OUT_ROWS, LANES), jnp.float32)
    real, imag = pl.pallas_call(
        add_far_kernel,
        out_shape=[jax.ShapeDtypeStruct((2 * PAIRS_DEV, 16, LANES), t) for t in (jnp.float32, SEND)],
        in_specs=[VMEM] * 4, out_specs=[VMEM] * 2, compiler_params=PARAMS,
    )(*along_y(far))
    near = pl.pallas_call(
        add_near_kernel, out_shape=[small] * 4, in_specs=[SMEM] + [VMEM] * 6, out_specs=[VMEM] * 4,
        compiler_params=PARAMS,
    )(ints, *along_y(near), move(real, dz=2), move(imag, dz=2))
    near = [near[0]] + [move(near[n], dx=n) for n in (1, 2, 3)]

    lane = np.arange(LANES)
    order = np.zeros((LANES, LANES), np.float32)
    order[lane, (lane // 64) * 64 + (lane % 32) * 2 + (lane // 32) % 2] = 1.0
    return pl.pallas_call(
        sum_kernel,
        out_shape=jax.ShapeDtypeStruct((PAIRS_DEV, 2048), jnp.float32),
        in_specs=[VMEM] * 5,
        out_specs=VMEM,
        scratch_shapes=[pltpu.VMEM((PAIRS_DEV * 16, LANES), jnp.float32)],
        compiler_params=PARAMS,
    )(*near, jnp.asarray(order))


def solution(mesh):
    placed = (P(None, "stn", "src"), P(None, "src"), P("src"), P("src"), P(), P(), P("stn", None))
    return jax.shard_map(
        body, mesh=mesh, in_specs=placed, out_specs=P("stn", "src"), check_vma=False
    )
```

```python
import functools
import math

import jax
import jax.numpy as jnp
import numpy as np
from jax import lax
from jax.experimental import pallas as pl
from jax.experimental.pallas import tpu as pltpu
from jax.sharding import PartitionSpec as P

NBLK = 16
STN = 8
PAIRS_DEV = 17
LANES = 128
JROWS = 512
EXTRA = 16
ROWS = JROWS + EXTRA
OUT_ROWS = PAIRS_DEV * 16
KCOL = 512
ACC = (2560, 256)

TWO_PI_HI = 6.28125
TWO_PI_LO = 2.0 * math.pi - 6.28125
def _fit(fun, power, terms):
    x = np.cos(np.pi * (np.arange(4000) + 0.5) / 4000) * (math.pi * 1.001)
    cols = np.stack([x ** (2 * n + power) for n in range(terms)], 1)
    scale = np.abs(cols).max(0)
    sol, *_ = np.linalg.lstsq(cols / scale, fun(x), rcond=None)
    return [float(v) for v in sol / scale]


SIN_TERMS = _fit(np.sin, 1, 7)
COS_TERMS = _fit(np.cos, 0, 8)


def horner(square, terms):
    total = jnp.full_like(square, terms[-1])
    for term in terms[-2::-1]:
        total = total * square + term
    return total


def three(rows, at):
    return (rows[at : at + 1] + rows[at + 1 : at + 2]) + rows[at + 2 : at + 3]


def split3(x):
    first = x.astype(jnp.bfloat16).astype(jnp.float32)
    second = (x - first).astype(jnp.bfloat16).astype(jnp.float32)
    return [first, second, x - first - second]


def prep_kernel(live_ref, lm_hbm, flux_hbm, pairs_hbm, jones_hbm, out_ref, *refs):
    lm_ref, flux_ref, pairs_ref, jones_ref, info_ref, sems = refs
    copies = [
        pltpu.make_async_copy(src, dst, sems.at[n])
        for n, (src, dst) in enumerate(
            ((jones_hbm, jones_ref), (lm_hbm, lm_ref), (flux_hbm, flux_ref), (pairs_hbm, pairs_ref))
        )
    ]
    for copy in copies:
        copy.start()
    for copy in copies[1:]:
        copy.wait()
    slots = jones_ref.shape[2]
    dir_l, dir_m = lm_ref[0:1, :], lm_ref[1:2, :]
    live = (lax.broadcasted_iota(jnp.int32, (1, slots), 1) < live_ref[0]).astype(jnp.float32)
    amp = jnp.sqrt(flux_ref[...] * live * (1.0 / math.sqrt(slots * 16)))
    depth = jnp.sqrt(1.0 - dir_l * dir_l - dir_m * dir_m) - 1.0
    info_ref[...] = jnp.zeros_like(info_ref)
    for n, row in enumerate((dir_l, dir_m, depth, amp)):
        for t, term in enumerate(split3(row)):
            info_ref[3 * n + t : 3 * n + t + 1, :] = term
    for d in range(STN):
        info_ref[12:14, LANES * d : LANES * d + PAIRS_DEV] = pairs_ref[...].astype(jnp.float32)
    copies[0].wait()
    src = lax.axis_index("src")
    first = 2 * (src // 4) + src % 2
    for d in range(STN):
        cols = pl.ds(pl.multiple_of((d + first) % STN * LANES, LANES), LANES)
        for comp in range(8):
            out_ref[d, 64 * comp : 64 * comp + 64, :] = jones_ref[comp, :, cols]
        out_ref[d, JROWS:ROWS, :] = info_ref[:, cols].astype(jnp.bfloat16)


def acc_at(tile, part):
    return 256 * (tile * (tile + 1) // 2) + 128 * (tile + 1) * part


def gram_piece(step, l_ref, g_ref, before_ref, acc_ref):
    tile, part = 3 - step // 2, step % 2
    rows = 128 * (tile + 1)
    at = acc_at(tile, part)
    got = lax.dot_general(
        l_ref[512 * part : 512 * part + rows, :], g_ref[256 * tile : 256 * tile + 256, :],
        (((1,), (1,)), ((), ())), preferred_element_type=jnp.float32,
    )
    acc_ref[at : at + rows, :] = got if before_ref is None else before_ref[at : at + rows, :] + got


def field_piece(stn, held, uvw_ref, scale, kappa, g_ref, l_ref):
    ref, at = (held[0], stn) if len(held) == 1 else (held[stn // 4], stn % 4)
    info = ref[0, JROWS:ROWS, :].astype(jnp.float32)
    dir_l, dir_m, depth, amp = (three(info, 3 * n) for n in range(4))
    for odd in range(2):
        blk = 2 * stn + odd
        here = slice(32 * blk, 32 * blk + 32)
        geometry = (uvw_ref[0, here, :] * dir_l + uvw_ref[1, here, :] * dir_m) + uvw_ref[2, here, :] * depth
        phase = scale * geometry
        turns = jnp.round(phase * (0.5 / math.pi))
        angle = (phase - turns * TWO_PI_HI) - turns * TWO_PI_LO
        square = angle * angle
        sine = horner(square, SIN_TERMS) * (angle * amp)
        cosine = horner(square, COS_TERMS) * amp
        for a in range(2):
            g_rows = slice(64 * blk + 32 * a, 64 * blk + 32 * a + 32)
            own = pl.ds(pl.multiple_of(64 * blk + 32 * a + 16 * kappa, 16), 16)
            l_re = slice(32 * blk + 16 * a, 32 * blk + 16 * a + 16)
            l_im = slice(512 + 32 * blk + 16 * a, 512 + 32 * blk + 16 * a + 16)
            for k in range(2):
                row = 64 * (2 * a + k) + 32 * odd
                real = ref[at, row : row + 32, :].astype(jnp.float32)
                imag = ref[at, 256 + row : 288 + row, :].astype(jnp.float32)
                c_re = slice(2 * k * LANES, (2 * k + 1) * LANES)
                c_im = slice((2 * k + 1) * LANES, (2 * k + 2) * LANES)
                g_ref[g_rows, c_re] = (real * cosine + imag * sine).astype(jnp.bfloat16)
                g_ref[g_rows, c_im] = (imag * cosine - real * sine).astype(jnp.bfloat16)
                x_re = g_ref[own, c_re]
                x_im = g_ref[own, c_im]
                l_ref[l_re, c_re] = x_re
                l_ref[l_re, c_im] = x_im
                l_ref[l_im, c_re] = x_im
                l_ref[l_im, c_im] = -x_re


def pack_pairs(acc_ref, idx_ref, out_ref):
    low = lax.broadcasted_iota(jnp.int32, (16, LANES), 1) < 64
    for i in range(NBLK):
        for tile in range(i // 2, NBLK // 2):
            cols = slice(LANES * (tile % 2), LANES * (tile % 2) + LANES)
            for part in range(2):
                top = acc_at(tile // 2, part) + 32 * i
                row0 = acc_ref[top : top + 16, cols]
                row1 = acc_ref[top + 16 : top + 32, cols]
                at = (part * NBLK + i) * NBLK + 2 * tile
                if i <= 2 * tile:
                    even = jnp.where(low, row0, pltpu.roll(row1, 64, 1))
                    out_ref[idx_ref[at]] = even.astype(out_ref.dtype)
                odd = jnp.where(low, pltpu.roll(row0, 64, 1), row1)
                out_ref[idx_ref[at + 1]] = odd.astype(out_ref.dtype)


def slab_kernel(chan, packs, chained, counts, *refs):
    scal_ref, int_ref, *refs = refs
    idx_ref = refs.pop(0) if packs else None
    uvw_ref, *refs = refs
    sets, source_refs = len(counts), []
    for count in counts:
        source_refs.append(refs[:count])
        refs = refs[count:]
    before_ref = refs.pop(0) if chained else None
    out_refs, refs = (refs[:4], refs[4:]) if packs else (refs[:1], refs[1:])
    acc_ref, held_ref, sems = refs[4:] if packs else (out_refs[0], None, None)
    work = (refs[0:2], refs[2:4])
    scale, kappa = scal_ref[chan], int_ref[0]
    for n in range(sets + 1):
        for step in range(STN):
            if n < sets:
                field_piece(step, source_refs[n], uvw_ref, scale, kappa, *work[n % 2])
            if n > 0:
                g_ref, l_ref = work[(n - 1) % 2]
                gram_piece(step, l_ref, g_ref, acc_ref if n > 1 else before_ref, acc_ref)
    if packs:
        pack_pairs(acc_ref, idx_ref, held_ref)
        each = 4 * PAIRS_DEV
        copies = [
            pltpu.make_async_copy(held_ref.at[each * n : each * n + each], out_ref, sems.at[n])
            for n, out_ref in enumerate(out_refs)
        ]
        for copy in copies:
            copy.start()
        for copy in copies:
            copy.wait()


def add_far_kernel(one, two, three, four, real_ref, imag_ref):
    total = one[...].astype(jnp.float32)
    for ref in (two, three, four):
        total = total + ref[...].astype(jnp.float32)
    real_ref[...] = total[: 2 * PAIRS_DEV]
    imag_ref[...] = total[2 * PAIRS_DEV :].astype(imag_ref.dtype)


def add_near_kernel(int_ref, one, two, three, four, real_ref, imag_ref, *outs):
    for n, out_ref in enumerate(outs):
        rows = slice(PAIRS_DEV * n, PAIRS_DEV * n + PAIRS_DEV)
        total = one[rows].astype(jnp.float32)
        for ref in (two, three, four):
            total = total + ref[rows].astype(jnp.float32)
        x_to = (int_ref[1] + n) % 4
        there = pl.ds(x_to % 2 * PAIRS_DEV, PAIRS_DEV)
        far = jnp.where(x_to < 2, real_ref[there], imag_ref[there].astype(jnp.float32))
        out_ref[...] = (total + far).reshape(out_ref.shape)


def sum_kernel(*refs):
    shares, (order_ref, out_ref, held_ref) = refs[:-3], refs[-3:]
    total = shares[0][...]
    for ref in shares[1:]:
        total = total + ref[...]
    held_ref[...] = jnp.dot(
        total, order_ref[...], precision=lax.Precision.HIGHEST, preferred_element_type=jnp.float32
    )
    for st in range(16):
        out_ref[:, LANES * st : LANES * st + LANES] = held_ref[pl.ds(st, PAIRS_DEV, stride=16), :]


VMEM = pl.BlockSpec(memory_space=pltpu.VMEM)
SMEM = pl.BlockSpec(memory_space=pltpu.SMEM)
PARAMS = pltpu.CompilerParams(vmem_limit_bytes=14 * 1024 * 1024)
ALONE = pltpu.CompilerParams(vmem_limit_bytes=62 * 1024 * 1024)
WORK = [pltpu.VMEM((1024, KCOL), jnp.bfloat16)] * 4
SEND = jnp.bfloat16


def coords():
    return [(xl, y, z, xh, core) for xl in range(2) for y in range(4) for z in range(4) for xh in range(2) for core in range(2)]


def place_of(xl, y, z, xh, core):
    return (xl * 4 + y % 4) * 16 + (z % 4) * 4 + xh * 2 + core


def move(x, dx=0, dy=0, dz=0, dcore=0, apart=0):
    perm = []
    for xl, y, z, xh, core in coords():
        x_to = (2 * xh + xl + dx) % 4
        z_to = z + dz + (apart if core == 0 else -apart)
        perm.append((place_of(xl, y, z, xh, core), place_of(x_to % 2, y + dy, z_to, x_to // 2, core ^ dcore)))
    return lax.ppermute(x, ("stn", "src"), perm)


def body(beam_jones, source_lm, source_flux, live_counts, station_uvw, chan_scale, block_pairs):
    src, stn = lax.axis_index("src"), lax.axis_index("stn")
    plane = src // 4
    x_own, y_own = 2 * ((src // 2) % 2) + stn // 4, stn % 4
    ints = jnp.stack([src % 2, x_own]).astype(jnp.int32)
    message = pl.pallas_call(
        prep_kernel,
        out_shape=jax.ShapeDtypeStruct((STN, ROWS, LANES), jnp.bfloat16),
        in_specs=[SMEM] + [pl.BlockSpec(memory_space=pl.ANY)] * 4,
        out_specs=VMEM,
        scratch_shapes=[
            pltpu.VMEM((2, STN * LANES), jnp.float32),
            pltpu.VMEM((1, STN * LANES), jnp.float32),
            pltpu.VMEM((2, PAIRS_DEV), jnp.int32),
            pltpu.VMEM((8, 64, STN * LANES), jnp.bfloat16),
            pltpu.VMEM((EXTRA, STN * LANES), jnp.float32),
            pltpu.SemaphoreType.DMA((4,)),
        ],
        compiler_params=ALONE,
    )(live_counts, source_lm, source_flux.reshape(1, -1), block_pairs.T, beam_jones)

    own = lax.all_to_all(message, "stn", 0, 0, tiled=True)
    got = [move(own[:4], apart=1), move(own[4:], apart=1)]
    other = move(own, dcore=1)
    other, chan_scale, station_uvw = lax.optimization_barrier((other, chan_scale, station_uvw))

    listed = other[:, JROWS + 12 : JROWS + 14, :PAIRS_DEV].astype(jnp.int32)
    holder = jnp.repeat(jnp.arange(STN, dtype=jnp.int32), PAIRS_DEV)
    slot = jnp.tile(jnp.arange(PAIRS_DEV, dtype=jnp.int32), STN)
    key = (listed[:, 0] * NBLK + listed[:, 1]).reshape(1, -1)
    hit = key == jnp.arange(NBLK * NBLK, dtype=jnp.int32)[:, None]
    part = jnp.arange(2, dtype=jnp.int32)[:, None]
    dy, dx = (holder % 4 - y_own) % 4, (2 * part + holder // 4 - x_own) % 4
    place = jnp.stack([dy * 4 + dx, dy * 4 + 2 * part + holder // 4]) * PAIRS_DEV + slot
    index = jnp.sum(jnp.where(hit[None, None], place[:, :, None, :], 0), axis=3).reshape(2, -1)

    scale = (2.0 * math.pi * chan_scale)[jnp.stack([plane, (plane + 2) % 4])]
    uvw = jnp.broadcast_to(station_uvw[:, :, None], (3, station_uvw.shape[1], LANES))

    square = jax.ShapeDtypeStruct(ACC, jnp.float32)
    packed = [jax.ShapeDtypeStruct((4 * PAIRS_DEV, 16, LANES), SEND)] * 4

    def slab(chan, packs, sources, before=None):
        chained = before is not None
        flat = [x for held in sources for x in held]
        return pl.pallas_call(
            functools.partial(slab_kernel, chan, packs, chained, [len(x) for x in sources]),
            out_shape=packed if packs else square,
            in_specs=[SMEM] * (3 if packs else 2) + [VMEM] * (1 + len(flat) + chained),
            out_specs=[pl.BlockSpec(memory_space=pl.ANY)] * 4 if packs else VMEM,
            scratch_shapes=WORK + ([
                pltpu.VMEM(ACC, jnp.float32), pltpu.VMEM((16 * PAIRS_DEV, 16, LANES), SEND), pltpu.SemaphoreType.DMA((4,))
            ] if packs else []),
            input_output_aliases={3 + len(flat): 0} if chained and not packs else {},
            compiler_params=PARAMS,
        )(scale, ints, *([index[chan]] if packs else []), uvw, *flat, *([before] if chained else []))

    def along_y(shares):
        return [shares[0]] + [move(shares[n], dy=n) for n in (1, 2, 3)]

    far = slab(1, False, [[own], [other]])
    near = slab(0, False, [[own], [other]])
    near, far, *got = lax.optimization_barrier((near, far, *got))
    other = [move(x, dcore=1) for x in got]
    far = slab(1, False, [got], far)
    far, *other = lax.optimization_barrier((far, *other))
    far = slab(1, True, [other], far)
    near, *far = lax.optimization_barrier((near, *far))
    near = slab(0, True, [got, other], near)
    small = jax.ShapeDtypeStruct((OUT_ROWS, LANES), jnp.float32)
    real, imag = pl.pallas_call(
        add_far_kernel,
        out_shape=[jax.ShapeDtypeStruct((2 * PAIRS_DEV, 16, LANES), t) for t in (jnp.float32, SEND)],
        in_specs=[VMEM] * 4, out_specs=[VMEM] * 2, compiler_params=PARAMS,
    )(*along_y(far))
    near = pl.pallas_call(
        add_near_kernel, out_shape=[small] * 4, in_specs=[SMEM] + [VMEM] * 6, out_specs=[VMEM] * 4,
        compiler_params=PARAMS,
    )(ints, *along_y(near), move(real, dz=2), move(imag, dz=2))
    near = [near[0]] + [move(near[n], dx=n) for n in (1, 2, 3)]

    lane = np.arange(LANES)
    order = np.zeros((LANES, LANES), np.float32)
    order[lane, (lane // 64) * 64 + (lane % 32) * 2 + (lane // 32) % 2] = 1.0
    return pl.pallas_call(
        sum_kernel,
        out_shape=jax.ShapeDtypeStruct((PAIRS_DEV, 2048), jnp.float32),
        in_specs=[VMEM] * 5,
        out_specs=VMEM,
        scratch_shapes=[pltpu.VMEM((PAIRS_DEV * 16, LANES), jnp.float32)],
        compiler_params=PARAMS,
    )(*near, jnp.asarray(order))


def solution(mesh):
    placed = (P(None, "stn", "src"), P(None, "src"), P("src"), P("src"), P(), P(), P("stn", None))
    return jax.shard_map(
        body, mesh=mesh, in_specs=placed, out_specs=P("stn", "src"), check_vma=False
    )
```

```python
import functools
import math

import jax
import jax.numpy as jnp
import numpy as np
from jax import lax
from jax.experimental import pallas as pl
from jax.experimental.pallas import tpu as pltpu
from jax.sharding import PartitionSpec as P

NBLK = 16
STN = 8
PAIRS_DEV = 17
LANES = 128
JROWS = 512
EXTRA = 16
ROWS = JROWS + EXTRA
OUT_ROWS = PAIRS_DEV * 16
KCOL = 512
ACC = (2560, 256)

TWO_PI_HI = 6.28125
TWO_PI_LO = 2.0 * math.pi - 6.28125
def _fit(fun, power, terms):
    x = np.cos(np.pi * (np.arange(4000) + 0.5) / 4000) * (math.pi * 1.001)
    cols = np.stack([x ** (2 * n + power) for n in range(terms)], 1)
    scale = np.abs(cols).max(0)
    sol, *_ = np.linalg.lstsq(cols / scale, fun(x), rcond=None)
    return [float(v) for v in sol / scale]


SIN_TERMS = _fit(np.sin, 1, 7)
COS_TERMS = _fit(np.cos, 0, 8)


def horner(square, terms):
    total = jnp.full_like(square, terms[-1])
    for term in terms[-2::-1]:
        total = total * square + term
    return total


def three(rows, at):
    return (rows[at : at + 1] + rows[at + 1 : at + 2]) + rows[at + 2 : at + 3]


def split3(x):
    first = x.astype(jnp.bfloat16).astype(jnp.float32)
    second = (x - first).astype(jnp.bfloat16).astype(jnp.float32)
    return [first, second, x - first - second]


def prep_kernel(live_ref, lm_hbm, flux_hbm, pairs_hbm, jones_hbm, out_hbm, *refs):
    lm_ref, flux_ref, pairs_ref, jones_ref, info_ref, out_ref, sems, out_sems = refs
    copies = [
        pltpu.make_async_copy(src, dst, sems.at[n])
        for n, (src, dst) in enumerate(
            ((jones_hbm, jones_ref), (lm_hbm, lm_ref), (flux_hbm, flux_ref), (pairs_hbm, pairs_ref))
        )
    ]
    for copy in copies:
        copy.start()
    for copy in copies[1:]:
        copy.wait()
    slots = jones_ref.shape[2]
    dir_l, dir_m = lm_ref[0:1, :], lm_ref[1:2, :]
    live = (lax.broadcasted_iota(jnp.int32, (1, slots), 1) < live_ref[0]).astype(jnp.float32)
    amp = jnp.sqrt(flux_ref[...] * live * (1.0 / math.sqrt(slots * 16)))
    depth = jnp.sqrt(1.0 - dir_l * dir_l - dir_m * dir_m) - 1.0
    info_ref[...] = jnp.zeros_like(info_ref)
    for n, row in enumerate((dir_l, dir_m, depth, amp)):
        for t, term in enumerate(split3(row)):
            info_ref[3 * n + t : 3 * n + t + 1, :] = term
    for d in range(STN):
        info_ref[12:14, LANES * d : LANES * d + PAIRS_DEV] = pairs_ref[...].astype(jnp.float32)
    copies[0].wait()
    src = lax.axis_index("src")
    first = 2 * (src // 4) + src % 2
    sent = []
    for d in range(STN):
        cols = pl.ds(pl.multiple_of((d + first) % STN * LANES, LANES), LANES)
        for comp in range(8):
            out_ref[d, 64 * comp : 64 * comp + 64, :] = jones_ref[comp, :, cols]
        out_ref[d, JROWS:ROWS, :] = info_ref[:, cols].astype(jnp.bfloat16)
        sent.append(pltpu.make_async_copy(out_ref.at[d], out_hbm.at[d], out_sems.at[d]))
        sent[-1].start()
    for copy in sent:
        copy.wait()


def acc_at(tile, part):
    return 256 * (tile * (tile + 1) // 2) + 128 * (tile + 1) * part


def gram_piece(step, l_ref, g_ref, before_ref, acc_ref):
    tile, part = 3 - step // 2, step % 2
    rows = 128 * (tile + 1)
    at = acc_at(tile, part)
    got = lax.dot_general(
        l_ref[512 * part : 512 * part + rows, :], g_ref[256 * tile : 256 * tile + 256, :],
        (((1,), (1,)), ((), ())), preferred_element_type=jnp.float32,
    )
    acc_ref[at : at + rows, :] = got if before_ref is None else before_ref[at : at + rows, :] + got


def field_piece(stn, held, uvw_ref, scale, kappa, g_ref, l_ref):
    ref, at = (held[0], stn) if len(held) == 1 else (held[stn // 4], stn % 4)
    info = ref[0, JROWS:ROWS, :].astype(jnp.float32)
    dir_l, dir_m, depth, amp = (three(info, 3 * n) for n in range(4))
    for odd in range(2):
        blk = 2 * stn + odd
        here = slice(32 * blk, 32 * blk + 32)
        geometry = (uvw_ref[0, here, :] * dir_l + uvw_ref[1, here, :] * dir_m) + uvw_ref[2, here, :] * depth
        phase = scale * geometry
        turns = jnp.round(phase * (0.5 / math.pi))
        angle = (phase - turns * TWO_PI_HI) - turns * TWO_PI_LO
        square = angle * angle
        sine = horner(square, SIN_TERMS) * (angle * amp)
        cosine = horner(square, COS_TERMS) * amp
        for a in range(2):
            g_rows = slice(64 * blk + 32 * a, 64 * blk + 32 * a + 32)
            own = pl.ds(pl.multiple_of(64 * blk + 32 * a + 16 * kappa, 16), 16)
            l_re = slice(32 * blk + 16 * a, 32 * blk + 16 * a + 16)
            l_im = slice(512 + 32 * blk + 16 * a, 512 + 32 * blk + 16 * a + 16)
            for k in range(2):
                row = 64 * (2 * a + k) + 32 * odd
                real = ref[at, row : row + 32, :].astype(jnp.float32)
                imag = ref[at, 256 + row : 288 + row, :].astype(jnp.float32)
                c_re = slice(2 * k * LANES, (2 * k + 1) * LANES)
                c_im = slice((2 * k + 1) * LANES, (2 * k + 2) * LANES)
                g_ref[g_rows, c_re] = (real * cosine + imag * sine).astype(jnp.bfloat16)
                g_ref[g_rows, c_im] = (imag * cosine - real * sine).astype(jnp.bfloat16)
                x_re = g_ref[own, c_re]
                x_im = g_ref[own, c_im]
                l_ref[l_re, c_re] = x_re
                l_ref[l_re, c_im] = x_im
                l_ref[l_im, c_re] = x_im
                l_ref[l_im, c_im] = -x_re


def pack_pairs(acc_ref, idx_ref, out_ref):
    low = lax.broadcasted_iota(jnp.int32, (16, LANES), 1) < 64
    for i in range(NBLK):
        for tile in range(i // 2, NBLK // 2):
            cols = slice(LANES * (tile % 2), LANES * (tile % 2) + LANES)
            for part in range(2):
                top = acc_at(tile // 2, part) + 32 * i
                row0 = acc_ref[top : top + 16, cols]
                row1 = acc_ref[top + 16 : top + 32, cols]
                at = (part * NBLK + i) * NBLK + 2 * tile
                if i <= 2 * tile:
                    even = jnp.where(low, row0, pltpu.roll(row1, 64, 1))
                    out_ref[idx_ref[at]] = even.astype(out_ref.dtype)
                odd = jnp.where(low, pltpu.roll(row0, 64, 1), row1)
                out_ref[idx_ref[at + 1]] = odd.astype(out_ref.dtype)


def slab_kernel(chan, packs, chained, counts, *refs):
    scal_ref, int_ref, *refs = refs
    idx_ref = refs.pop(0) if packs else None
    uvw_ref, *refs = refs
    sets, source_refs = len(counts), []
    for count in counts:
        source_refs.append(refs[:count])
        refs = refs[count:]
    before_ref = refs.pop(0) if chained else None
    out_refs, refs = (refs[:4], refs[4:]) if packs else (refs[:1], refs[1:])
    acc_ref, held_ref, sems = refs[4:] if packs else (out_refs[0], None, None)
    work = (refs[0:2], refs[2:4])
    scale, kappa = scal_ref[chan], int_ref[0]
    for n in range(sets + 1):
        for step in range(STN):
            if n < sets:
                field_piece(step, source_refs[n], uvw_ref, scale, kappa, *work[n % 2])
            if n > 0:
                g_ref, l_ref = work[(n - 1) % 2]
                gram_piece(step, l_ref, g_ref, acc_ref if n > 1 else before_ref, acc_ref)
    if packs:
        pack_pairs(acc_ref, idx_ref, held_ref)
        each = 4 * PAIRS_DEV
        copies = [
            pltpu.make_async_copy(held_ref.at[each * n : each * n + each], out_ref, sems.at[n])
            for n, out_ref in enumerate(out_refs)
        ]
        for copy in copies:
            copy.start()
        for copy in copies:
            copy.wait()


def add_far_kernel(one, two, three, four, real_ref, imag_ref):
    total = one[...].astype(jnp.float32)
    for ref in (two, three, four):
        total = total + ref[...].astype(jnp.float32)
    real_ref[...] = total[: 2 * PAIRS_DEV]
    imag_ref[...] = total[2 * PAIRS_DEV :].astype(imag_ref.dtype)


def add_near_kernel(int_ref, one, two, three, four, real_ref, imag_ref, *outs):
    for n, out_ref in enumerate(outs):
        rows = slice(PAIRS_DEV * n, PAIRS_DEV * n + PAIRS_DEV)
        total = one[rows].astype(jnp.float32)
        for ref in (two, three, four):
            total = total + ref[rows].astype(jnp.float32)
        x_to = (int_ref[1] + n) % 4
        there = pl.ds(x_to % 2 * PAIRS_DEV, PAIRS_DEV)
        far = jnp.where(x_to < 2, real_ref[there], imag_ref[there].astype(jnp.float32))
        out_ref[...] = (total + far).reshape(out_ref.shape)


def sum_kernel(*refs):
    shares, (order_ref, out_ref, held_ref) = refs[:-3], refs[-3:]
    total = shares[0][...]
    for ref in shares[1:]:
        total = total + ref[...]
    held_ref[...] = jnp.dot(
        total, order_ref[...], precision=lax.Precision.HIGHEST, preferred_element_type=jnp.float32
    )
    for st in range(16):
        out_ref[:, LANES * st : LANES * st + LANES] = held_ref[pl.ds(st, PAIRS_DEV, stride=16), :]


VMEM = pl.BlockSpec(memory_space=pltpu.VMEM)
SMEM = pl.BlockSpec(memory_space=pltpu.SMEM)
PARAMS = pltpu.CompilerParams(vmem_limit_bytes=14 * 1024 * 1024)
ALONE = pltpu.CompilerParams(vmem_limit_bytes=62 * 1024 * 1024)
WORK = [pltpu.VMEM((1024, KCOL), jnp.bfloat16)] * 4
SEND = jnp.bfloat16


def coords():
    return [(xl, y, z, xh, core) for xl in range(2) for y in range(4) for z in range(4) for xh in range(2) for core in range(2)]


def place_of(xl, y, z, xh, core):
    return (xl * 4 + y % 4) * 16 + (z % 4) * 4 + xh * 2 + core


def move(x, dx=0, dy=0, dz=0, dcore=0, apart=0):
    perm = []
    for xl, y, z, xh, core in coords():
        x_to = (2 * xh + xl + dx) % 4
        z_to = z + dz + (apart if core == 0 else -apart)
        perm.append((place_of(xl, y, z, xh, core), place_of(x_to % 2, y + dy, z_to, x_to // 2, core ^ dcore)))
    return lax.ppermute(x, ("stn", "src"), perm)


def body(beam_jones, source_lm, source_flux, live_counts, station_uvw, chan_scale, block_pairs):
    src, stn = lax.axis_index("src"), lax.axis_index("stn")
    plane = src // 4
    x_own, y_own = 2 * ((src // 2) % 2) + stn // 4, stn % 4
    ints = jnp.stack([src % 2, x_own]).astype(jnp.int32)
    message = pl.pallas_call(
        prep_kernel,
        out_shape=jax.ShapeDtypeStruct((STN, ROWS, LANES), jnp.bfloat16),
        in_specs=[SMEM] + [pl.BlockSpec(memory_space=pl.ANY)] * 4,
        out_specs=pl.BlockSpec(memory_space=pl.ANY),
        scratch_shapes=[
            pltpu.VMEM((2, STN * LANES), jnp.float32),
            pltpu.VMEM((1, STN * LANES), jnp.float32),
            pltpu.VMEM((2, PAIRS_DEV), jnp.int32),
            pltpu.VMEM((8, 64, STN * LANES), jnp.bfloat16),
            pltpu.VMEM((EXTRA, STN * LANES), jnp.float32),
            pltpu.VMEM((STN, ROWS, LANES), jnp.bfloat16),
            pltpu.SemaphoreType.DMA((4,)),
            pltpu.SemaphoreType.DMA((STN,)),
        ],
        compiler_params=ALONE,
    )(live_counts, source_lm, source_flux.reshape(1, -1), block_pairs.T, beam_jones)

    own = lax.all_to_all(message, "stn", 0, 0, tiled=True)
    got = [move(own[:4], apart=1), move(own[4:], apart=1)]
    other = move(own, dcore=1)
    other, chan_scale, station_uvw = lax.optimization_barrier((other, chan_scale, station_uvw))

    listed = other[:, JROWS + 12 : JROWS + 14, :PAIRS_DEV].astype(jnp.int32)
    holder = jnp.repeat(jnp.arange(STN, dtype=jnp.int32), PAIRS_DEV)
    slot = jnp.tile(jnp.arange(PAIRS_DEV, dtype=jnp.int32), STN)
    key = (listed[:, 0] * NBLK + listed[:, 1]).reshape(1, -1)
    hit = key == jnp.arange(NBLK * NBLK, dtype=jnp.int32)[:, None]
    part = jnp.arange(2, dtype=jnp.int32)[:, None]
    dy, dx = (holder % 4 - y_own) % 4, (2 * part + holder // 4 - x_own) % 4
    place = jnp.stack([dy * 4 + dx, dy * 4 + 2 * part + holder // 4]) * PAIRS_DEV + slot
    index = jnp.sum(jnp.where(hit[None, None], place[:, :, None, :], 0), axis=3).reshape(2, -1)

    scale = (2.0 * math.pi * chan_scale)[jnp.stack([plane, (plane + 2) % 4])]
    uvw = jnp.broadcast_to(station_uvw[:, :, None], (3, station_uvw.shape[1], LANES))

    square = jax.ShapeDtypeStruct(ACC, jnp.float32)
    packed = [jax.ShapeDtypeStruct((4 * PAIRS_DEV, 16, LANES), SEND)] * 4

    def slab(chan, packs, sources, before=None):
        chained = before is not None
        flat = [x for held in sources for x in held]
        return pl.pallas_call(
            functools.partial(slab_kernel, chan, packs, chained, [len(x) for x in sources]),
            out_shape=packed if packs else square,
            in_specs=[SMEM] * (3 if packs else 2) + [VMEM] * (1 + len(flat) + chained),
            out_specs=[pl.BlockSpec(memory_space=pl.ANY)] * 4 if packs else VMEM,
            scratch_shapes=WORK + ([
                pltpu.VMEM(ACC, jnp.float32), pltpu.VMEM((16 * PAIRS_DEV, 16, LANES), SEND), pltpu.SemaphoreType.DMA((4,))
            ] if packs else []),
            input_output_aliases={3 + len(flat): 0} if chained and not packs else {},
            compiler_params=PARAMS,
        )(scale, ints, *([index[chan]] if packs else []), uvw, *flat, *([before] if chained else []))

    def along_y(shares):
        return [shares[0]] + [move(shares[n], dy=n) for n in (1, 2, 3)]

    far = slab(1, False, [[own], [other]])
    near = slab(0, False, [[own], [other]])
    near, far, *got = lax.optimization_barrier((near, far, *got))
    other = [move(x, dcore=1) for x in got]
    far = slab(1, False, [got], far)
    far, *other = lax.optimization_barrier((far, *other))
    far = slab(1, True, [other], far)
    near, *far = lax.optimization_barrier((near, *far))
    near = slab(0, True, [got, other], near)
    small = jax.ShapeDtypeStruct((OUT_ROWS, LANES), jnp.float32)
    real, imag = pl.pallas_call(
        add_far_kernel,
        out_shape=[jax.ShapeDtypeStruct((2 * PAIRS_DEV, 16, LANES), t) for t in (jnp.float32, SEND)],
        in_specs=[VMEM] * 4, out_specs=[VMEM] * 2, compiler_params=PARAMS,
    )(*along_y(far))
    near = pl.pallas_call(
        add_near_kernel, out_shape=[small] * 4, in_specs=[SMEM] + [VMEM] * 6, out_specs=[VMEM] * 4,
        compiler_params=PARAMS,
    )(ints, *along_y(near), move(real, dz=2), move(imag, dz=2))
    near = [near[0]] + [move(near[n], dx=n) for n in (1, 2, 3)]

    lane = np.arange(LANES)
    order = np.zeros((LANES, LANES), np.float32)
    order[lane, (lane // 64) * 64 + (lane % 32) * 2 + (lane // 32) % 2] = 1.0
    return pl.pallas_call(
        sum_kernel,
        out_shape=jax.ShapeDtypeStruct((PAIRS_DEV, 2048), jnp.float32),
        in_specs=[VMEM] * 5,
        out_specs=VMEM,
        scratch_shapes=[pltpu.VMEM((PAIRS_DEV * 16, LANES), jnp.float32)],
        compiler_params=PARAMS,
    )(*near, jnp.asarray(order))


def solution(mesh):
    placed = (P(None, "stn", "src"), P(None, "src"), P("src"), P("src"), P(), P(), P("stn", None))
    return jax.shard_map(
        body, mesh=mesh, in_specs=placed, out_specs=P("stn", "src"), check_vma=False
    )
```

```python
import functools
import math

import jax
import jax.numpy as jnp
import numpy as np
from jax import lax
from jax.experimental import pallas as pl
from jax.experimental.pallas import tpu as pltpu
from jax.sharding import PartitionSpec as P

NBLK = 16
STN = 8
PAIRS_DEV = 17
LANES = 128
JROWS = 512
EXTRA = 16
ROWS = JROWS + EXTRA
OUT_ROWS = PAIRS_DEV * 16
KCOL = 512
ACC = (2560, 256)

TWO_PI_HI = 6.28125
TWO_PI_LO = 2.0 * math.pi - 6.28125
def _fit(fun, power, terms):
    x = np.cos(np.pi * (np.arange(4000) + 0.5) / 4000) * (math.pi * 1.001)
    cols = np.stack([x ** (2 * n + power) for n in range(terms)], 1)
    scale = np.abs(cols).max(0)
    sol, *_ = np.linalg.lstsq(cols / scale, fun(x), rcond=None)
    return [float(v) for v in sol / scale]


SIN_TERMS = _fit(np.sin, 1, 7)
COS_TERMS = _fit(np.cos, 0, 8)


def horner(square, terms):
    total = jnp.full_like(square, terms[-1])
    for term in terms[-2::-1]:
        total = total * square + term
    return total


def three(rows, at):
    return (rows[at : at + 1] + rows[at + 1 : at + 2]) + rows[at + 2 : at + 3]


def split3(x):
    first = x.astype(jnp.bfloat16).astype(jnp.float32)
    second = (x - first).astype(jnp.bfloat16).astype(jnp.float32)
    return [first, second, x - first - second]


def prep_kernel(live_ref, lm_hbm, flux_hbm, pairs_hbm, jones_hbm, out_hbm, *refs):
    lm_ref, flux_ref, pairs_ref, jones_ref, info_ref, out_ref, sems, out_sems = refs
    copies = [
        pltpu.make_async_copy(src, dst, sems.at[n])
        for n, (src, dst) in enumerate(
            ((jones_hbm, jones_ref), (lm_hbm, lm_ref), (flux_hbm, flux_ref), (pairs_hbm, pairs_ref))
        )
    ]
    for copy in copies:
        copy.start()
    for copy in copies[1:]:
        copy.wait()
    slots = jones_ref.shape[2]
    dir_l, dir_m = lm_ref[0:1, :], lm_ref[1:2, :]
    live = (lax.broadcasted_iota(jnp.int32, (1, slots), 1) < live_ref[0]).astype(jnp.float32)
    amp = jnp.sqrt(flux_ref[...] * live * (1.0 / math.sqrt(slots * 16)))
    depth = jnp.sqrt(1.0 - dir_l * dir_l - dir_m * dir_m) - 1.0
    info_ref[...] = jnp.zeros_like(info_ref)
    for n, row in enumerate((dir_l, dir_m, depth, amp)):
        for t, term in enumerate(split3(row)):
            info_ref[3 * n + t : 3 * n + t + 1, :] = term
    for d in range(STN):
        info_ref[12:14, LANES * d : LANES * d + PAIRS_DEV] = pairs_ref[...].astype(jnp.float32)
    copies[0].wait()
    src = lax.axis_index("src")
    first = 2 * (src // 4) + src % 2
    sent = []
    for d in range(STN):
        cols = pl.ds(pl.multiple_of((d + first) % STN * LANES, LANES), LANES)
        for comp in range(8):
            out_ref[d, 64 * comp : 64 * comp + 64, :] = jones_ref[comp, :, cols]
        out_ref[d, JROWS:ROWS, :] = info_ref[:, cols].astype(jnp.bfloat16)
        sent.append(pltpu.make_async_copy(out_ref.at[d], out_hbm.at[d], out_sems.at[d]))
        sent[-1].start()
    for copy in sent:
        copy.wait()


def acc_at(tile, part):
    return 256 * (tile * (tile + 1) // 2) + 128 * (tile + 1) * part


def gram_piece(step, l_ref, g_ref, before_ref, acc_ref):
    tile, part = 3 - step // 2, step % 2
    rows = 128 * (tile + 1)
    at = acc_at(tile, part)
    got = lax.dot_general(
        l_ref[512 * part : 512 * part + rows, :], g_ref[256 * tile : 256 * tile + 256, :],
        (((1,), (1,)), ((), ())), preferred_element_type=jnp.float32,
    )
    acc_ref[at : at + rows, :] = got if before_ref is None else before_ref[at : at + rows, :] + got


def field_piece(stn, held, uvw_ref, scale, kappa, g_ref, l_ref):
    ref, at = (held[0], stn) if len(held) == 1 else (held[stn // 4], stn % 4)
    info = ref[0, JROWS:ROWS, :].astype(jnp.float32)
    dir_l, dir_m, depth, amp = (three(info, 3 * n) for n in range(4))
    for odd in range(2):
        blk = 2 * stn + odd
        here = slice(32 * blk, 32 * blk + 32)
        geometry = (uvw_ref[0, here, :] * dir_l + uvw_ref[1, here, :] * dir_m) + uvw_ref[2, here, :] * depth
        phase = scale * geometry
        turns = jnp.round(phase * (0.5 / math.pi))
        angle = (phase - turns * TWO_PI_HI) - turns * TWO_PI_LO
        square = angle * angle
        sine = horner(square, SIN_TERMS) * (angle * amp)
        cosine = horner(square, COS_TERMS) * amp
        for a in range(2):
            g_rows = slice(64 * blk + 32 * a, 64 * blk + 32 * a + 32)
            own = pl.ds(pl.multiple_of(64 * blk + 32 * a + 16 * kappa, 16), 16)
            l_re = slice(32 * blk + 16 * a, 32 * blk + 16 * a + 16)
            l_im = slice(512 + 32 * blk + 16 * a, 512 + 32 * blk + 16 * a + 16)
            for k in range(2):
                row = 64 * (2 * a + k) + 32 * odd
                real = ref[at, row : row + 32, :].astype(jnp.float32)
                imag = ref[at, 256 + row : 288 + row, :].astype(jnp.float32)
                c_re = slice(2 * k * LANES, (2 * k + 1) * LANES)
                c_im = slice((2 * k + 1) * LANES, (2 * k + 2) * LANES)
                g_ref[g_rows, c_re] = (real * cosine + imag * sine).astype(jnp.bfloat16)
                g_ref[g_rows, c_im] = (imag * cosine - real * sine).astype(jnp.bfloat16)
                x_re = g_ref[own, c_re]
                x_im = g_ref[own, c_im]
                l_ref[l_re, c_re] = x_re
                l_ref[l_re, c_im] = x_im
                l_ref[l_im, c_re] = x_im
                l_ref[l_im, c_im] = -x_re


def pack_pairs(acc_ref, idx_ref, out_ref):
    low = lax.broadcasted_iota(jnp.int32, (16, LANES), 1) < 64
    for i in range(NBLK):
        for tile in range(i // 2, NBLK // 2):
            cols = slice(LANES * (tile % 2), LANES * (tile % 2) + LANES)
            for part in range(2):
                top = acc_at(tile // 2, part) + 32 * i
                row0 = acc_ref[top : top + 16, cols]
                row1 = acc_ref[top + 16 : top + 32, cols]
                at = (part * NBLK + i) * NBLK + 2 * tile
                if i <= 2 * tile:
                    even = jnp.where(low, row0, pltpu.roll(row1, 64, 1))
                    out_ref[idx_ref[at]] = even.astype(out_ref.dtype)
                odd = jnp.where(low, pltpu.roll(row0, 64, 1), row1)
                out_ref[idx_ref[at + 1]] = odd.astype(out_ref.dtype)


def slab_kernel(chan, packs, chained, counts, *refs):
    scal_ref, int_ref, *refs = refs
    idx_ref = refs.pop(0) if packs else None
    uvw_ref, *refs = refs
    sets, source_refs = len(counts), []
    for count in counts:
        source_refs.append(refs[:count])
        refs = refs[count:]
    before_ref = refs.pop(0) if chained else None
    out_refs, refs = (refs[:4], refs[4:]) if packs else (refs[:1], refs[1:])
    acc_ref, held_ref, sems = refs[4:] if packs else (out_refs[0], None, None)
    work = (refs[0:2], refs[2:4])
    scale, kappa = scal_ref[chan], int_ref[0]
    for n in range(sets + 1):
        for step in range(STN):
            if n < sets:
                field_piece(step, source_refs[n], uvw_ref, scale, kappa, *work[n % 2])
            if n > 0:
                g_ref, l_ref = work[(n - 1) % 2]
                gram_piece(step, l_ref, g_ref, acc_ref if n > 1 else before_ref, acc_ref)
    if packs:
        pack_pairs(acc_ref, idx_ref, held_ref)
        each = 4 * PAIRS_DEV
        copies = [
            pltpu.make_async_copy(held_ref.at[each * n : each * n + each], out_ref, sems.at[n])
            for n, out_ref in enumerate(out_refs)
        ]
        for copy in copies:
            copy.start()
        for copy in copies:
            copy.wait()


def add_far_kernel(one, two, three, four, real_ref, imag_ref):
    total = one[...].astype(jnp.float32)
    for ref in (two, three, four):
        total = total + ref[...].astype(jnp.float32)
    real_ref[...] = total[: 2 * PAIRS_DEV]
    imag_ref[...] = total[2 * PAIRS_DEV :].astype(imag_ref.dtype)


def add_near_kernel(int_ref, one, two, three, four, real_ref, imag_ref, *outs):
    for n, out_ref in enumerate(outs):
        rows = slice(PAIRS_DEV * n, PAIRS_DEV * n + PAIRS_DEV)
        total = one[rows].astype(jnp.float32)
        for ref in (two, three, four):
            total = total + ref[rows].astype(jnp.float32)
        x_to = (int_ref[1] + n) % 4
        there = pl.ds(x_to % 2 * PAIRS_DEV, PAIRS_DEV)
        far = jnp.where(x_to < 2, real_ref[there], imag_ref[there].astype(jnp.float32))
        out_ref[...] = (total + far).reshape(out_ref.shape)


def sum_kernel(*refs):
    shares, (order_ref, out_ref, held_ref) = refs[:-3], refs[-3:]
    total = shares[0][...]
    for ref in shares[1:]:
        total = total + ref[...]
    held_ref[...] = jnp.dot(
        total, order_ref[...], precision=lax.Precision.HIGHEST, preferred_element_type=jnp.float32
    )
    for st in range(16):
        out_ref[:, LANES * st : LANES * st + LANES] = held_ref[pl.ds(st, PAIRS_DEV, stride=16), :]


VMEM = pl.BlockSpec(memory_space=pltpu.VMEM)
SMEM = pl.BlockSpec(memory_space=pltpu.SMEM)
PARAMS = pltpu.CompilerParams(vmem_limit_bytes=14 * 1024 * 1024)
ALONE = pltpu.CompilerParams(vmem_limit_bytes=62 * 1024 * 1024)
WORK = [pltpu.VMEM((1024, KCOL), jnp.bfloat16)] * 4
SEND = jnp.bfloat16


def coords():
    return [(xl, y, z, xh, core) for xl in range(2) for y in range(4) for z in range(4) for xh in range(2) for core in range(2)]


def place_of(xl, y, z, xh, core):
    return (xl * 4 + y % 4) * 16 + (z % 4) * 4 + xh * 2 + core


def move(x, dx=0, dy=0, dz=0, dcore=0, apart=0):
    perm = []
    for xl, y, z, xh, core in coords():
        x_to = (2 * xh + xl + dx) % 4
        z_to = z + dz + (apart if core == 0 else -apart)
        perm.append((place_of(xl, y, z, xh, core), place_of(x_to % 2, y + dy, z_to, x_to // 2, core ^ dcore)))
    return lax.ppermute(x, ("stn", "src"), perm)


def body(beam_jones, source_lm, source_flux, live_counts, station_uvw, chan_scale, block_pairs):
    src, stn = lax.axis_index("src"), lax.axis_index("stn")
    plane = src // 4
    x_own, y_own = 2 * ((src // 2) % 2) + stn // 4, stn % 4
    ints = jnp.stack([src % 2, x_own]).astype(jnp.int32)
    message = pl.pallas_call(
        prep_kernel,
        out_shape=jax.ShapeDtypeStruct((STN, ROWS, LANES), jnp.bfloat16),
        in_specs=[SMEM] + [pl.BlockSpec(memory_space=pl.ANY)] * 4,
        out_specs=pl.BlockSpec(memory_space=pl.ANY),
        scratch_shapes=[
            pltpu.VMEM((2, STN * LANES), jnp.float32),
            pltpu.VMEM((1, STN * LANES), jnp.float32),
            pltpu.VMEM((2, PAIRS_DEV), jnp.int32),
            pltpu.VMEM((8, 64, STN * LANES), jnp.bfloat16),
            pltpu.VMEM((EXTRA, STN * LANES), jnp.float32),
            pltpu.VMEM((STN, ROWS, LANES), jnp.bfloat16),
            pltpu.SemaphoreType.DMA((4,)),
            pltpu.SemaphoreType.DMA((STN,)),
        ],
        compiler_params=ALONE,
    )(live_counts, source_lm, source_flux.reshape(1, -1), block_pairs.T, beam_jones)

    own = lax.all_to_all(message, "stn", 0, 0, tiled=True)
    got = [move(own[:4], apart=1), move(own[4:], apart=1)]
    other = move(own, dcore=1)
    other, chan_scale, station_uvw = lax.optimization_barrier((other, chan_scale, station_uvw))

    listed = other[:, JROWS + 12 : JROWS + 14, :PAIRS_DEV].astype(jnp.int32)
    holder = jnp.repeat(jnp.arange(STN, dtype=jnp.int32), PAIRS_DEV)
    slot = jnp.tile(jnp.arange(PAIRS_DEV, dtype=jnp.int32), STN)
    key = (listed[:, 0] * NBLK + listed[:, 1]).reshape(1, -1)
    hit = key == jnp.arange(NBLK * NBLK, dtype=jnp.int32)[:, None]
    part = jnp.arange(2, dtype=jnp.int32)[:, None]
    dy, dx = (holder % 4 - y_own) % 4, (2 * part + holder // 4 - x_own) % 4
    place = jnp.stack([dy * 4 + dx, dy * 4 + 2 * part + holder // 4]) * PAIRS_DEV + slot
    index = jnp.sum(jnp.where(hit[None, None], place[:, :, None, :], 0), axis=3).reshape(2, -1)

    scale = (2.0 * math.pi * chan_scale)[jnp.stack([plane, (plane + 2) % 4])]
    uvw = jnp.broadcast_to(station_uvw[:, :, None], (3, station_uvw.shape[1], LANES))

    square = jax.ShapeDtypeStruct(ACC, jnp.float32)
    packed = [jax.ShapeDtypeStruct((4 * PAIRS_DEV, 16, LANES), SEND)] * 4

    def slab(chan, packs, sources, before=None):
        chained = before is not None
        flat = [x for held in sources for x in held]
        return pl.pallas_call(
            functools.partial(slab_kernel, chan, packs, chained, [len(x) for x in sources]),
            out_shape=packed if packs else square,
            in_specs=[SMEM] * (3 if packs else 2) + [VMEM] * (1 + len(flat) + chained),
            out_specs=[pl.BlockSpec(memory_space=pl.ANY)] * 4 if packs else VMEM,
            scratch_shapes=WORK + ([
                pltpu.VMEM(ACC, jnp.float32), pltpu.VMEM((16 * PAIRS_DEV, 16, LANES), SEND), pltpu.SemaphoreType.DMA((4,))
            ] if packs else []),
            input_output_aliases={3 + len(flat): 0} if chained and not packs else {},
            compiler_params=PARAMS,
        )(scale, ints, *([index[chan]] if packs else []), uvw, *flat, *([before] if chained else []))

    def along_y(shares):
        moved = {n: move(shares[n], dy=n) for n in (2, 1, 3)}
        return [shares[0]] + [moved[n] for n in (1, 2, 3)]

    far = slab(1, False, [[own], [other]])
    near = slab(0, False, [[own], [other]])
    near, far, *got = lax.optimization_barrier((near, far, *got))
    other = [move(x, dcore=1) for x in got]
    far = slab(1, False, [got], far)
    far, *other = lax.optimization_barrier((far, *other))
    far = slab(1, True, [other], far)
    near, *far = lax.optimization_barrier((near, *far))
    near = slab(0, True, [got, other], near)
    small = jax.ShapeDtypeStruct((OUT_ROWS, LANES), jnp.float32)
    real, imag = pl.pallas_call(
        add_far_kernel,
        out_shape=[jax.ShapeDtypeStruct((2 * PAIRS_DEV, 16, LANES), t) for t in (jnp.float32, SEND)],
        in_specs=[VMEM] * 4, out_specs=[VMEM] * 2, compiler_params=PARAMS,
    )(*along_y(far))
    near = pl.pallas_call(
        add_near_kernel, out_shape=[small] * 4, in_specs=[SMEM] + [VMEM] * 6, out_specs=[VMEM] * 4,
        compiler_params=PARAMS,
    )(ints, *along_y(near), move(real, dz=2), move(imag, dz=2))
    near = [near[0]] + [move(near[n], dx=n) for n in (2, 1, 3)]

    lane = np.arange(LANES)
    order = np.zeros((LANES, LANES), np.float32)
    order[lane, (lane // 64) * 64 + (lane % 32) * 2 + (lane // 32) % 2] = 1.0
    return pl.pallas_call(
        sum_kernel,
        out_shape=jax.ShapeDtypeStruct((PAIRS_DEV, 2048), jnp.float32),
        in_specs=[VMEM] * 5,
        out_specs=VMEM,
        scratch_shapes=[pltpu.VMEM((PAIRS_DEV * 16, LANES), jnp.float32)],
        compiler_params=PARAMS,
    )(*near, jnp.asarray(order))


def solution(mesh):
    placed = (P(None, "stn", "src"), P(None, "src"), P("src"), P("src"), P(), P(), P("stn", None))
    return jax.shard_map(
        body, mesh=mesh, in_specs=placed, out_specs=P("stn", "src"), check_vma=False
    )
```
